256 devices in a mesh: gx: 8 (over z), gy: 32 (over y, x, core).
Axes of the slice: x: 4, y: 4, z: 8, core: 2. Of those that a mesh axis runs over, the one named last changes fastest.
Arguments:
- start_charges: float32 [65536, 128], P(('gx', 'gy'))
- solute_field: float32 [65536, 128], P(('gx', 'gy'))
- exposure: float32 [65536, 128], P(('gx', 'gy')), may hold values from 0 to 1
- owner_offset: int32 [65536, 32], P(('gx', 'gy')), may hold values from 0 to 8, as said below
- owner_row: int32 [65536, 32], P(('gx', 'gy')), may hold values from 0 to 255, as said below
- live_slots: int32 [65536, 4], P(('gx', 'gy')), may hold values from 0 to 8
- coupling: float32 [65536, 32], P(('gx', 'gy')), may hold values from 0.02 to 0.2
- cell_index: int32 [65536], P(('gx', 'gy')), may hold values from 0 to 1023, never falling along the last dimension, each value on 1 to 128 neighbouring positions
- evaluation: float32 [512, 128], replicated
- projection: float32 [128, 128], replicated
- far_kernel: float32 [1024, 1024], replicated, may hold values from -0.01171875 to 0.01171875
Outputs:
- final_charges: float32 [65536, 128], P(('gx', 'gy'))
The draws below stay inside these ranges and needn't reach their ends.
Inputs may be any that keep to these rules, and one draw needn't show every extreme that they name: `owner_offset`: A neighbour lies on the sphere's own device (offset 4) or on a device beside it or across a corner in the 8 x 32 grid of devices; no offset leaves the grid. `owner_row`: A neighbour on another device is among the first 64 spheres of that device. `cell_index`: cell numbers never fall along the spheres; each cell holds 1 to 128 spheres.
All inputs are finite; a program needn't handle non-finite values.
Results may differ from the reference program's by a relative error of at most 0.0003.
Values sent between devices are 32-bit elements; how exact they have to be, the bound alone decides.
A program may use at most 64 MiB of HBM per device.

```python
import math
import jax
import jax.numpy as jnp
import numpy as np
from jax import lax

LMAX = 10
H = 128
LEB = 110
G = 128
Q = 16
ND = 4
SLOTS = 8
NB = 32
SPH_DEV = 256
EDGE = 64
CELL_DEV = 4
ITERS = 4
NS = 65536
NC = 1024
N_GX = 8
N_GY = 32


def harmonic_mask():
    return (jnp.arange(H) < (LMAX + 1) ** 2).astype(jnp.float32)


def neighbour_draw(key):
    sphere = jnp.arange(NS, dtype=jnp.int32)
    device = sphere // SPH_DEV
    place_x = device // N_GY
    place_y = device % N_GY
    key_one, key_two, key_three, key_four = jax.random.split(key, 4)
    staying = jax.random.randint(key_one, (NS, NB), 0, 2)
    wanted = jax.random.randint(key_two, (NS, NB), 0, 9)
    direction = jnp.where(staying == 0, 4, wanted)
    target_x = place_x[:, None] + direction // 3 - 1
    target_y = place_y[:, None] + direction % 3 - 1
    inside = (target_x >= 0) & (target_x < N_GX) & (target_y >= 0) & (target_y < N_GY)
    direction = jnp.where(inside, direction, 4)
    near_row = jax.random.randint(key_three, (NS, NB), 0, SPH_DEV)
    edge_row = jax.random.randint(key_four, (NS, NB), 0, EDGE)
    row_value = jnp.where(direction == 4, near_row, edge_row)
    direction = direction.at[0, 0].set(4)
    row_value = row_value.at[0, 0].set(SPH_DEV - 1)
    direction = direction.at[0, 1].set(8)
    row_value = row_value.at[0, 1].set(EDGE - 1)
    direction = direction.at[NS - 1, 1].set(0)
    row_value = row_value.at[NS - 1, 1].set(0)
    return (direction.astype(jnp.int32), row_value.astype(jnp.int32))


def draw_owner_offset(key, part):
    direction, row_value = neighbour_draw(key)
    return direction


def draw_owner_row(key, part):
    direction, row_value = neighbour_draw(key)
    return row_value


def draw_live_slots(key, part):
    key = jax.random.fold_in(key, 5)
    key_one, key_two, key_three = jax.random.split(key, 3)
    devices = NS // SPH_DEV
    dense = jax.random.randint(key_one, (devices,), 0, 4) == 0
    dense = dense.at[0].set(True)
    dense_rows = jnp.repeat(dense, SPH_DEV)
    heavy = jax.random.randint(key_two, (NS, ND), 6, SLOTS + 1)
    light = jax.random.randint(key_three, (NS, ND), 0, 5)
    values = jnp.where(dense_rows[:, None], heavy, light)
    values = values.at[0, :].set(SLOTS)
    return values.astype(jnp.int32)


def draw_start_charges(key, part):
    key = jax.random.fold_in(key, 1)
    key_one = jax.random.fold_in(key, 0)
    values = jax.random.normal(key_one, (NS, H), jnp.float32)
    return values * harmonic_mask()[None, :]


def draw_solute_field(key, part):
    key = jax.random.fold_in(key, 2)
    key_one, key_two = jax.random.split(key)
    rising = jnp.exp(math.log(3.0) * jnp.arange(NS, dtype=jnp.float32) / NS) / 1.7
    values = jax.random.normal(key_one, (NS, H), jnp.float32)
    values = values * jnp.exp(jax.random.uniform(key_two, (NS, 1), jnp.float32, 0.0, math.log(10.0))) / 3.0
    return values * rising[:, None]


def draw_evaluation(key, part):
    key = jax.random.fold_in(key, 3)
    values = jax.random.normal(key, (ND * H, G), jnp.float32)
    row_mask = harmonic_mask()[jnp.arange(ND * H) % H]
    column_mask = (jnp.arange(G) < LEB).astype(jnp.float32)
    return values * row_mask[:, None] * column_mask[None, :] / math.sqrt(ND * (LMAX + 1) ** 2)


def draw_projection(key, part):
    key = jax.random.fold_in(key, 4)
    values = jax.random.normal(key, (G, H), jnp.float32)
    row_mask = (jnp.arange(G) < LEB).astype(jnp.float32)
    return values * row_mask[:, None] * harmonic_mask()[None, :] / math.sqrt(LEB)


def block_scale(rng, dims, cuts, low, top_value):
    loudness = 1.0
    for position, shards_of in cuts:
        steps = jax.random.uniform(jax.random.fold_in(jax.random.fold_in(rng, 6), position), (shards_of,), jnp.float32, low / len(cuts), top_value / len(cuts))
        loudness = loudness * jnp.repeat(jnp.exp(steps), dims[position] // shards_of).reshape((-1,) + (1,) * (len(dims) - 1 - position))
    return loudness


def length_profile(amount, total, most, lean):
    weights = [(1 << 20) // math.isqrt(rank ** lean) + 1 for rank in range(2, amount + 1)]
    surplus, holding = total - most - (amount - 1), [1] * (amount - 1)
    while surplus > 0:
        candidates = [i for i in range(amount - 1) if holding[i] < most]
        mass, left = sum([weights[i] for i in candidates]), surplus
        for i in candidates:
            addition = min(most - holding[i], max(1, left * weights[i] // mass), surplus)
            holding[i] = holding[i] + addition
            surplus = surplus - addition
    return np.array([most] + holding)


def ragged(stream_key, number_of, total, reach, slope):
    if number_of == 2:
        one = jax.random.randint(stream_key, (), max(1, total - reach), min(reach, total - 1) + 1)
        return jnp.stack([one, total - one])
    sizes = jnp.asarray(length_profile(number_of, total, reach, slope), jnp.int32)
    twos = (number_of - 1) // 2
    source_of, taker = sizes[1:1 + 2 * twos:2], sizes[2:2 + 2 * twos:2]
    room = jnp.minimum(source_of - 1, reach - taker)
    moved = jax.random.randint(jax.random.fold_in(stream_key, 1), (twos,), 0, 1 << 20) % (room + 1)
    sizes = sizes.at[1:1 + 2 * twos:2].set(source_of - moved).at[2:2 + 2 * twos:2].set(taker + moved)
    return sizes[jax.random.permutation(jax.random.fold_in(stream_key, 2), number_of)]


def gaussian(rng, shape, scale, most, held_as=jnp.bfloat16):
    entries = jax.random.normal(rng, shape, jnp.float32) * scale
    return jnp.minimum(jnp.maximum(entries, -most), most).astype(held_as)


def setup_inputs(seed: int = 0) -> dict:
    keys = jax.random.split(jax.random.key(seed), 12)
    start_charges = draw_start_charges(jax.random.fold_in(keys[11], 71), 0)
    solute_field = draw_solute_field(jax.random.fold_in(keys[11], 71), 0)
    exposure = jnp.clip(1.0 * jax.random.uniform(keys[2], (NS, G), jnp.float32) ** block_scale(keys[2], (NS, G), ((0, 256),), -0.2, 0.2), 0.0, 1.0)
    owner_offset = draw_owner_offset(jax.random.fold_in(keys[11], 71), 0)
    owner_row = draw_owner_row(jax.random.fold_in(keys[11], 71), 0)
    live_slots = draw_live_slots(jax.random.fold_in(keys[11], 71), 0)
    coupling = jnp.clip(jnp.exp(math.log(0.2) - 2.3025851 * jax.random.uniform(keys[6], (NS, NB), jnp.float32) ** block_scale(keys[6], (NS, NB), ((0, 256),), -0.2, 0.2)), 0.02, 0.2)
    cell_index = jnp.searchsorted(jnp.cumsum(ragged(keys[7], NC, NS, 2 * SPH_DEV // CELL_DEV, 0)), jnp.arange(NS), side="right").astype(jnp.int32)
    evaluation = draw_evaluation(jax.random.fold_in(keys[11], 71), 0)
    projection = draw_projection(jax.random.fold_in(keys[11], 71), 0)
    far_kernel = gaussian(keys[10], (NC, NC), (4 * NS) ** -0.5, 0.01171875, jnp.float32)
    return dict(start_charges=start_charges, solute_field=solute_field, exposure=exposure, owner_offset=owner_offset, owner_row=owner_row, live_slots=live_slots, coupling=coupling, cell_index=cell_index, evaluation=evaluation, projection=projection, far_kernel=far_kernel)


def degree_scale():
    index = jnp.arange(H, dtype=jnp.int32)
    bounds = jnp.arange(1, LMAX + 1, dtype=jnp.int32) ** 2
    degree = lax.optimization_barrier(jnp.sum((index[:, None] >= bounds[None, :]).astype(jnp.int32), axis=1))
    values = (2.0 * degree.astype(jnp.float32) + 1.0) / (4.0 * math.pi)
    return jnp.where(index < (LMAX + 1) ** 2, values, jnp.float32(0.0)).astype(jnp.float32)

def spd_mixing(margins):
    order = len(margins)
    diagonal_sum = margins[0][0]
    for a in range(1, order):
        diagonal_sum = diagonal_sum + margins[a][a]
    damping = 0.01 * diagonal_sum / order
    triangle = [[None] * order for a in range(order)]
    for a in range(order):
        for b in range(a + 1):
            running = margins[a][b] + (damping if a == b else 0.0)
            for c in range(b):
                running = running - triangle[a][c] * triangle[b][c]
            if a == b:
                triangle[a][a] = jnp.sqrt(running)
            else:
                triangle[a][b] = running / triangle[b][b]
    forward = []
    for a in range(order):
        running = jnp.float32(1.0)
        for c in range(a):
            running = running - triangle[a][c] * forward[c]
        forward.append(running / triangle[a][a])
    backward = [None] * order
    for a in reversed(range(order)):
        running = forward[a]
        for c in range(a + 1, order):
            running = running - triangle[c][a] * backward[c]
        backward[a] = running / triangle[a][a]
    weight_sum = backward[0]
    for a in range(1, order):
        weight_sum = weight_sum + backward[a]
    return [value / weight_sum for value in backward]

def reference(start_charges, solute_field, exposure, owner_offset, owner_row, live_slots, coupling, cell_index, evaluation, projection, far_kernel):
    highest = lax.Precision.HIGHEST
    scale = degree_scale()
    sphere = jnp.arange(NS, dtype=jnp.int32)
    device = sphere // SPH_DEV
    place_x = device // N_GY
    place_y = device % N_GY
    other = (place_x[:, None] + owner_offset // 3 - 1) * N_GY + place_y[:, None] + owner_offset % 3 - 1
    targets = (other * SPH_DEV + owner_row).astype(jnp.int32)
    slot_index = jnp.arange(NB, dtype=jnp.int32) % SLOTS
    live = slot_index[None, :] < jnp.repeat(live_slots, SLOTS, axis=1)
    weights = jnp.where(live, coupling, jnp.float32(0.0)).astype(jnp.float32)

    def jacobi_map(charges):
        blocks = []
        for d in range(ND):
            running = jnp.zeros((NS, H), jnp.float32)
            for s in range(SLOTS):
                column = d * SLOTS + s
                running = running + weights[:, column][:, None] * charges[targets[:, column]]
            blocks.append(running)
        classes = jnp.concatenate(blocks, axis=1)
        potential = jnp.dot(classes, evaluation, precision=highest)
        nearby = jnp.dot(potential * exposure, projection, precision=highest)
        moments = jax.ops.segment_sum(charges[:, :Q], cell_index, num_segments=NC)
        expansion = jnp.dot(far_kernel.T, moments, precision=highest)
        distant = jnp.pad(expansion[cell_index], ((0, 0), (0, H - Q)))
        return scale[None, :] * (solute_field - nearby - distant)
    charges = start_charges
    history = []
    changes = []
    rows_list = []
    for t in range(ITERS):
        updated = jacobi_map(charges)
        change = updated - charges
        history.append(updated)
        changes.append(change)
        rows_list.append([jnp.sum(change * other_change) for other_change in changes])
        margins = [[rows_list[max(a, b)][min(a, b)] for b in range(t + 1)] for a in range(t + 1)]
        mixing = spd_mixing(margins)
        charges = mixing[0] * history[0]
        for a in range(1, t + 1):
            charges = charges + mixing[a] * history[a]
    return charges
```

```python
import functools
import math

import jax
import jax.numpy as jnp
from jax import lax
from jax.experimental import pallas as pl
from jax.experimental.pallas import tpu as pltpu
from jax.sharding import PartitionSpec as P

MESH = pl.DeviceIdType.MESH
F32 = jnp.float32
BF16 = jnp.bfloat16

LMAX = 10
H = 128
Q = 16
ND = 4
SLOTS = 8
NB = 32
EDGE = 64
ITERS = 4
SPH = 256
NC = 1024
SRC = SPH + 8 * EDGE
LANES = 128
TILES = NC // LANES
AROUND = [(dx, dy) for dx in (-1, 0, 1) for dy in (-1, 0, 1) if (dx, dy) != (0, 0)]
NN = (((1,), (0,)), ((), ()))
NT = (((1,), (1,)), ((), ()))


def spd_mixing(margins):
    order = len(margins)
    diagonal_sum = margins[0][0]
    for a in range(1, order):
        diagonal_sum = diagonal_sum + margins[a][a]
    damping = 0.01 * diagonal_sum / order
    triangle = [[None] * order for a in range(order)]
    for a in range(order):
        for b in range(a + 1):
            running = margins[a][b] + (damping if a == b else 0.0)
            for c in range(b):
                running = running - triangle[a][c] * triangle[b][c]
            if a == b:
                triangle[a][a] = jnp.sqrt(running)
            else:
                triangle[a][b] = running / triangle[b][b]
    forward = []
    for a in range(order):
        running = jnp.ones_like(diagonal_sum)
        for c in range(a):
            running = running - triangle[a][c] * forward[c]
        forward.append(running / triangle[a][a])
    backward = [None] * order
    for a in reversed(range(order)):
        running = forward[a]
        for c in range(a + 1, order):
            running = running - triangle[c][a] * backward[c]
        backward[a] = running / triangle[a][a]
    weight_sum = backward[0]
    for a in range(1, order):
        weight_sum = weight_sum + backward[a]
    return [value / weight_sum for value in backward]


def split(value):
    high = value.astype(BF16)
    return high, (value - high.astype(F32)).astype(BF16)


def dot(a, b, dims=NN):
    return lax.dot_general(a, b, dims, preferred_element_type=F32)


def total(value):
    rows = jnp.sum(value.reshape(-1, 8, LANES), axis=0)
    return jnp.sum(jnp.sum(rows, axis=0, keepdims=True), axis=1, keepdims=True)


def largest(value):
    rows = jnp.max(value.reshape(-1, 8, LANES), axis=0)
    return jnp.max(jnp.max(rows, axis=0, keepdims=True), axis=1, keepdims=True)


def mixed_coefficients(gram):
    zero = jnp.zeros_like(gram[0][0])
    one = jnp.ones_like(zero)
    rhos = [[one] + [zero] * ITERS]
    margins = []
    for t in range(ITERS):
        new = rhos[t]
        image = []
        for l in range(ITERS):
            running = None
            for k in range(t + 1):
                term = new[k] * gram[max(k, l)][min(k, l)]
                running = term if running is None else running + term
            image.append(running)
        row = []
        for a in range(t + 1):
            running = None
            for l in range(a + 1):
                term = rhos[a][l] * image[l]
                running = term if running is None else running + term
            row.append(running)
        margins.append(row)
        full = [[margins[max(a, b)][min(a, b)] for b in range(t + 1)] for a in range(t + 1)]
        mixing = spd_mixing(full)
        following = [zero]
        for k in range(ITERS):
            running = zero
            for a in range(t + 1):
                if k <= a:
                    running = running + mixing[a] * rhos[a][k]
            following.append(running)
        rhos.append(following)
    return rhos[ITERS]


def kernel(
    n_gx,
    n_gy,
    x_hbm,
    solute_ref,
    exposure_ref,
    offset_ref,
    row_ref,
    live_ref,
    coupling_ref,
    cell_ref,
    evaluation_ref,
    projection_ref,
    far_hbm,
    out_ref,
    y,
    far,
    whigh,
    wlow,
    classes,
    member,
    onehot,
    kghigh,
    kglow,
    halo,
    mine,
    part_in,
    plane,
    mid_in,
    whole,
    moments,
    gram_out,
    gram_in,
    gram_mid,
    gram_mid_in,
    load_sem,
    halo_send,
    halo_recv,
    part_send,
    part_recv,
    mid_send,
    mid_recv,
    whole_send,
    whole_recv,
    gram_send,
    gram_recv,
):
    gx = lax.axis_index("gx")
    gy = lax.axis_index("gy")
    piece = LANES // n_gy

    def peer_y(step):
        return (gx, lax.rem(gy + step, n_gy))

    def peer_x(step):
        return (lax.rem(gx + step, n_gx), gy)

    def beside(index):
        dx, dy = AROUND[index]
        return (lax.rem(gx + dx + n_gx, n_gx), lax.rem(gy + dy + n_gy, n_gy))

    barrier = pltpu.get_barrier_semaphore()

    def greet_y(step, carry):
        pl.semaphore_signal(barrier, inc=1, device_id=peer_y(step), device_id_type=MESH)
        return carry

    def greet_x(step, carry):
        pl.semaphore_signal(barrier, inc=1, device_id=peer_x(step), device_id_type=MESH)
        return carry

    load_x = pltpu.make_async_copy(x_hbm, y.at[0], load_sem.at[0])
    load_far = pltpu.make_async_copy(far_hbm, far, load_sem.at[1])
    load_x.start()
    load_far.start()
    lax.fori_loop(1, n_gy, greet_y, 0)
    lax.fori_loop(1, n_gx, greet_x, 0)
    corners = [i for i, (dx, dy) in enumerate(AROUND) if dx != 0 and dy != 0]
    for i in corners:
        pl.semaphore_signal(barrier, inc=1, device_id=beside(i), device_id_type=MESH)

    cell_row = jnp.broadcast_to(cell_ref[...], (LANES, SPH))
    for t in range(TILES):
        cells = lax.broadcasted_iota(jnp.int32, (LANES, SPH), 0) + t * LANES
        member[t * LANES : (t + 1) * LANES, :] = (cell_row == cells).astype(F32).astype(BF16)
    cell_column = cell_row.astype(F32).T
    for t in range(TILES):
        cells = (lax.broadcasted_iota(jnp.int32, (SPH, LANES), 1) + t * LANES).astype(F32)
        onehot[:, t * LANES : (t + 1) * LANES] = (cell_column == cells).astype(F32).astype(BF16)

    def halo_copy(k, index):
        return pltpu.make_async_remote_copy(
            src_ref=y.at[k, pl.ds(0, EDGE)],
            dst_ref=halo.at[k, pl.ds((7 - index) * EDGE, EDGE)],
            send_sem=halo_send.at[k, index],
            recv_sem=halo_recv.at[k, 7 - index],
            device_id=beside(index),
            device_id_type=MESH,
        )

    def part_copy(k, step):
        return pltpu.make_async_remote_copy(
            src_ref=mine.at[k, lax.rem(gy + step, n_gy)],
            dst_ref=part_in.at[k, step],
            send_sem=part_send.at[k],
            recv_sem=part_recv.at[k],
            device_id=peer_y(step),
            device_id_type=MESH,
        )

    def mid_copy(k, step):
        return pltpu.make_async_remote_copy(
            src_ref=plane.at[k],
            dst_ref=mid_in.at[k, step],
            send_sem=mid_send.at[k],
            recv_sem=mid_recv.at[k],
            device_id=peer_x(step),
            device_id_type=MESH,
        )

    def whole_copy(k, step):
        return pltpu.make_async_remote_copy(
            src_ref=whole.at[k, gy],
            dst_ref=whole.at[k, gy],
            send_sem=whole_send.at[k],
            recv_sem=whole_recv.at[k],
            device_id=peer_y(step),
            device_id_type=MESH,
        )

    def gram_copy_y(step):
        return pltpu.make_async_remote_copy(
            src_ref=gram_out.at[0],
            dst_ref=gram_in.at[step],
            send_sem=gram_send.at[0],
            recv_sem=gram_recv.at[0],
            device_id=peer_y(step),
            device_id_type=MESH,
        )

    def gram_copy_x(step):
        return pltpu.make_async_remote_copy(
            src_ref=gram_mid.at[0],
            dst_ref=gram_mid_in.at[step],
            send_sem=gram_send.at[1],
            recv_sem=gram_recv.at[1],
            device_id=peer_x(step),
            device_id_type=MESH,
        )

    def send_all(copy, count):
        def one(step, carry):
            copy(step).start()
            return carry

        lax.fori_loop(1, count, one, 0)

    def bytes_of(ref, sem):
        return pltpu.make_async_copy(ref, ref, sem)

    def begin(k):
        for index in range(8):
            halo_copy(k, index).start()
        first = y[k].T[:Q]
        high, rest = split(first)
        lows = first - high.astype(F32)
        middle, last = split(lows)
        stacked = jnp.concatenate([high, middle, last], axis=0)
        parts = dot(stacked, member[...], NT)
        parts = parts[:Q] + parts[Q : 2 * Q] + parts[2 * Q :]
        per = Q // min(piece, Q)
        for t in range(TILES):
            block = parts[:, t * LANES : (t + 1) * LANES]
            if piece >= Q:
                each = piece // Q
                mine[k, t // each, (t % each) * Q : (t % each + 1) * Q, :] = block
            else:
                for j in range(per):
                    mine[k, t * per + j] = block[j * piece : (j + 1) * piece]
        send_all(functools.partial(part_copy, k), n_gy)

    load_x.wait()
    pl.semaphore_wait(barrier, (n_gy - 1) + (n_gx - 1) + len(corners))
    begin(0)

    block_rows = 16

    def weigh(step, carry):
        base = pl.multiple_of(step * block_rows, block_rows)
        offs = offset_ref[pl.ds(base, block_rows), :]
        owner = row_ref[pl.ds(base, block_rows), :]
        place = jnp.where(
            offs == 4, owner, SPH + jnp.where(offs > 4, offs - 1, offs) * EDGE + owner
        )
        alive = live_ref[pl.ds(base, block_rows), :]
        margin = coupling_ref[pl.ds(base, block_rows), :]
        columns = lax.broadcasted_iota(jnp.int32, (block_rows, SRC), 1)
        for d in range(ND):
            weights = jnp.zeros((block_rows, SRC), F32)
            for s in range(SLOTS):
                slot = d * SLOTS + s
                value = jnp.where(
                    s < alive[:, d : d + 1], margin[:, slot : slot + 1], jnp.float32(0.0)
                )
                weights = weights + jnp.where(
                    place[:, slot : slot + 1] == columns, value, jnp.float32(0.0)
                )
            high, low = split(weights)
            rows = pl.ds(pl.multiple_of(d * SPH + base, block_rows), block_rows)
            whigh[rows, :] = high
            wlow[rows, :] = low
        return carry

    lax.fori_loop(0, SPH // block_rows, weigh, 0)

    load_far.wait()
    for t in range(TILES):
        high, low = split(far[t * LANES : (t + 1) * LANES, :])
        kghigh[:, t * LANES : (t + 1) * LANES] = dot(onehot[...], high, NT).astype(BF16)
        kglow[:, t * LANES : (t + 1) * LANES] = dot(onehot[...], low, NT).astype(BF16)

    index = lax.broadcasted_iota(jnp.int32, (1, H), 1)
    degree = jnp.zeros((1, H), F32)
    for n in range(1, LMAX + 1):
        degree = degree + (index >= n * n).astype(F32)
    scale = jnp.where(index < (LMAX + 1) ** 2, (2.0 * degree + 1.0) / (4.0 * math.pi), 0.0)
    evaluation_parts = jnp.concatenate(split(evaluation_ref[...]), axis=1)
    projection_parts = jnp.concatenate(split(projection_ref[...]), axis=1)

    def product(left, right):
        high, low = split(left)
        both = dot(high, right)
        return both[:, :H] + both[:, H:] + dot(low, right[:, :H])

    def near_part(d, columns, source):
        rows = pl.ds(d * SPH, SPH)
        both = dot(whigh[rows, columns], source)
        return both[:, :H] + both[:, H:] + dot(wlow[rows, columns], source[:, :H])

    def iterate(k, carry):
        own = jnp.concatenate(split(y[k]), axis=1)
        for d in range(ND):
            classes[:, d * H : (d + 1) * H] = near_part(d, pl.ds(0, SPH), own)

        bytes_of(part_in.at[k, pl.ds(1, n_gy - 1)], part_recv.at[k]).wait()
        plane[k] = jnp.sum(part_in[k, 1:], axis=0) + mine[k, gy]
        send_all(functools.partial(mid_copy, k), n_gx)

        for i in range(8):
            halo_copy(k, i).wait_recv()
        others = jnp.concatenate(split(halo[k]), axis=1)
        for d in range(ND):
            classes[:, d * H : (d + 1) * H] += near_part(d, pl.ds(SPH, 8 * EDGE), others)

        bytes_of(mid_in.at[k, pl.ds(1, n_gx - 1)], mid_recv.at[k]).wait()
        whole[k, gy] = jnp.sum(mid_in[k, 1:], axis=0) + plane[k]
        send_all(functools.partial(whole_copy, k), n_gy)

        potential = product(classes[...], evaluation_parts)
        nearby = product(potential * exposure_ref[...], projection_parts)
        near = solute_ref[...] - nearby

        bytes_of(whole.at[k, pl.ds(0, n_gy - 1)], whole_recv.at[k]).wait()
        for t in range(TILES):
            columns = slice(t * LANES, (t + 1) * LANES)
            if piece >= Q:
                each = piece // Q
                moments[:, columns] = whole[k, t // each, (t % each) * Q : (t % each + 1) * Q, :]
            else:
                per = Q // piece
                for j in range(per):
                    moments[j * piece : (j + 1) * piece, columns] = whole[k, t * per + j]
        high, low = split(moments[...])
        blank = jnp.zeros((H - Q, NC), BF16)
        both = jnp.concatenate([high, blank, low, blank], axis=0)
        far_both = dot(kghigh[...], both, NT)
        distant = far_both[:, :H] + far_both[:, H:] + dot(kglow[...], both[:H], NT)
        y[k + 1] = scale * (near - distant)

        @pl.when(k < ITERS - 1)
        def _():
            begin(k + 1)

        for i in range(8):
            halo_copy(k, i).wait_send()
        sent = pl.ds(0, n_gy - 1)
        bytes_of(mine.at[k, sent], part_send.at[k]).wait()
        bytes_of(mid_in.at[k, pl.ds(1, n_gx - 1)], mid_send.at[k]).wait()
        bytes_of(whole.at[k, sent], whole_send.at[k]).wait()
        return carry

    lax.fori_loop(0, ITERS, iterate, 0)

    changes = [y[k + 1] - y[k] for k in range(ITERS)]
    height = jnp.abs(changes[0])
    for k in range(1, ITERS):
        height = jnp.maximum(height, jnp.abs(changes[k]))
    top = largest(height)
    top = jnp.where(top > 0.0, top, 1.0)
    inverse = 1.0 / top
    changes = [change * inverse for change in changes]
    lane = lax.broadcasted_iota(jnp.int32, (1, LANES), 1)
    pairs = [(a, b) for a in range(ITERS) for b in range(a + 1)]
    line = jnp.where(lane == len(pairs), top, 0.0)
    for i, (a, b) in enumerate(pairs):
        line = line + jnp.where(lane == i, total(changes[a] * changes[b]), 0.0)

    def merged(lines):
        tops = lines[:, len(pairs) : len(pairs) + 1]
        most = jnp.max(tops, axis=0, keepdims=True)
        ratio = tops / most
        sums = jnp.sum(lines * (ratio * ratio), axis=0, keepdims=True)
        return jnp.where(lane == len(pairs), most, sums)

    gram_out[0] = line
    gram_in[0] = line
    send_all(gram_copy_y, n_gy)
    bytes_of(gram_in.at[pl.ds(1, n_gy - 1)], gram_recv.at[0]).wait()
    line = merged(gram_in[...].reshape(n_gy, LANES))
    gram_mid[0] = line
    gram_mid_in[0] = line
    send_all(gram_copy_x, n_gx)
    bytes_of(gram_mid_in.at[pl.ds(1, n_gx - 1)], gram_recv.at[1]).wait()
    line = merged(gram_mid_in[...].reshape(n_gx, LANES))

    gram = [[None] * ITERS for a in range(ITERS)]
    for i, (a, b) in enumerate(pairs):
        gram[a][b] = line[:, i : i + 1]
    rho = mixed_coefficients(gram)
    mixed = rho[1] * y[1]
    for k in range(2, ITERS + 1):
        mixed = mixed + rho[k] * y[k]
    out_ref[...] = mixed

    bytes_of(gram_in.at[pl.ds(1, n_gy - 1)], gram_send.at[0]).wait()
    bytes_of(gram_mid_in.at[pl.ds(1, n_gx - 1)], gram_send.at[1]).wait()


def per_device(
    n_gx,
    n_gy,
    start_charges,
    solute_field,
    exposure,
    owner_offset,
    owner_row,
    live_slots,
    coupling,
    cell_index,
    evaluation,
    projection,
    far_kernel,
):
    vmem = pl.BlockSpec(memory_space=pltpu.VMEM)
    hbm = pl.BlockSpec(memory_space=pl.ANY)
    piece = LANES // n_gy
    dma = pltpu.SemaphoreType.DMA
    return pl.pallas_call(
        functools.partial(kernel, n_gx, n_gy),
        out_shape=jax.ShapeDtypeStruct((SPH, H), F32),
        in_specs=[hbm] + [vmem] * 9 + [hbm],
        out_specs=vmem,
        scratch_shapes=[
            pltpu.VMEM((ITERS + 1, SPH, H), F32),
            pltpu.VMEM((NC, NC), F32),
            pltpu.VMEM((ND * SPH, SRC), BF16),
            pltpu.VMEM((ND * SPH, SRC), BF16),
            pltpu.VMEM((SPH, ND * H), F32),
            pltpu.VMEM((NC, SPH), BF16),
            pltpu.VMEM((SPH, NC), BF16),
            pltpu.VMEM((SPH, NC), BF16),
            pltpu.VMEM((SPH, NC), BF16),
            pltpu.VMEM((ITERS, 8 * EDGE, H), F32),
            pltpu.VMEM((ITERS, n_gy, piece, LANES), F32),
            pltpu.VMEM((ITERS, n_gy, piece, LANES), F32),
            pltpu.VMEM((ITERS, piece, LANES), F32),
            pltpu.VMEM((ITERS, n_gx, piece, LANES), F32),
            pltpu.VMEM((ITERS, n_gy, piece, LANES), F32),
            pltpu.VMEM((Q, NC), F32),
            pltpu.VMEM((1, 1, LANES), F32),
            pltpu.VMEM((n_gy, 1, LANES), F32),
            pltpu.VMEM((1, 1, LANES), F32),
            pltpu.VMEM((n_gx, 1, LANES), F32),
            dma((2,)),
            dma((ITERS, 8)),
            dma((ITERS, 8)),
            dma((ITERS,)),
            dma((ITERS,)),
            dma((ITERS,)),
            dma((ITERS,)),
            dma((ITERS,)),
            dma((ITERS,)),
            dma((2,)),
            dma((2,)),
        ],
        compiler_params=pltpu.CompilerParams(
            collective_id=0, has_side_effects=True, vmem_limit_bytes=48 * 1024 * 1024
        ),
        name="screening",
    )(
        start_charges,
        solute_field,
        exposure,
        owner_offset,
        owner_row,
        live_slots,
        coupling,
        cell_index.reshape(1, SPH),
        evaluation,
        projection,
        far_kernel,
    )


def solution(mesh):
    placed = (
        P(("gx", "gy"), None),
        P(("gx", "gy"), None),
        P(("gx", "gy"), None),
        P(("gx", "gy"), None),
        P(("gx", "gy"), None),
        P(("gx", "gy"), None),
        P(("gx", "gy"), None),
        P(("gx", "gy")),
        P(),
        P(),
        P(),
    )
    return jax.shard_map(
        functools.partial(per_device, mesh.shape["gx"], mesh.shape["gy"]),
        mesh=mesh,
        in_specs=placed,
        out_specs=P(("gx", "gy"), None),
        check_vma=False,
    )
```

```python
import functools
import math

import jax
import jax.numpy as jnp
from jax import lax
from jax.experimental import pallas as pl
from jax.experimental.pallas import tpu as pltpu
from jax.sharding import PartitionSpec as P

MESH = pl.DeviceIdType.MESH
F32 = jnp.float32
BF16 = jnp.bfloat16

LMAX = 10
H = 128
Q = 16
ND = 4
SLOTS = 8
NB = 32
EDGE = 64
ITERS = 4
SPH = 256
NC = 1024
SRC = SPH + 8 * EDGE
LANES = 128
TILES = NC // LANES
AROUND = [(dx, dy) for dx in (-1, 0, 1) for dy in (-1, 0, 1) if (dx, dy) != (0, 0)]
NN = (((1,), (0,)), ((), ()))
NT = (((1,), (1,)), ((), ()))


def spd_mixing(margins):
    order = len(margins)
    diagonal_sum = margins[0][0]
    for a in range(1, order):
        diagonal_sum = diagonal_sum + margins[a][a]
    damping = 0.01 * diagonal_sum / order
    triangle = [[None] * order for a in range(order)]
    for a in range(order):
        for b in range(a + 1):
            running = margins[a][b] + (damping if a == b else 0.0)
            for c in range(b):
                running = running - triangle[a][c] * triangle[b][c]
            if a == b:
                triangle[a][a] = jnp.sqrt(running)
            else:
                triangle[a][b] = running / triangle[b][b]
    forward = []
    for a in range(order):
        running = jnp.ones_like(diagonal_sum)
        for c in range(a):
            running = running - triangle[a][c] * forward[c]
        forward.append(running / triangle[a][a])
    backward = [None] * order
    for a in reversed(range(order)):
        running = forward[a]
        for c in range(a + 1, order):
            running = running - triangle[c][a] * backward[c]
        backward[a] = running / triangle[a][a]
    weight_sum = backward[0]
    for a in range(1, order):
        weight_sum = weight_sum + backward[a]
    return [value / weight_sum for value in backward]


def split(value):
    high = value.astype(BF16)
    return high, (value - high.astype(F32)).astype(BF16)


def dot(a, b, dims=NN):
    return lax.dot_general(a, b, dims, preferred_element_type=F32)


def total(value):
    rows = jnp.sum(value.reshape(-1, 8, LANES), axis=0)
    return jnp.sum(jnp.sum(rows, axis=0, keepdims=True), axis=1, keepdims=True)


def largest(value):
    rows = jnp.max(value.reshape(-1, 8, LANES), axis=0)
    return jnp.max(jnp.max(rows, axis=0, keepdims=True), axis=1, keepdims=True)


def mixed_coefficients(gram):
    zero = jnp.zeros_like(gram[0][0])
    one = jnp.ones_like(zero)
    rhos = [[one] + [zero] * ITERS]
    margins = []
    for t in range(ITERS):
        new = rhos[t]
        image = []
        for l in range(ITERS):
            running = None
            for k in range(t + 1):
                term = new[k] * gram[max(k, l)][min(k, l)]
                running = term if running is None else running + term
            image.append(running)
        row = []
        for a in range(t + 1):
            running = None
            for l in range(a + 1):
                term = rhos[a][l] * image[l]
                running = term if running is None else running + term
            row.append(running)
        margins.append(row)
        full = [[margins[max(a, b)][min(a, b)] for b in range(t + 1)] for a in range(t + 1)]
        mixing = spd_mixing(full)
        following = [zero]
        for k in range(ITERS):
            running = zero
            for a in range(t + 1):
                if k <= a:
                    running = running + mixing[a] * rhos[a][k]
            following.append(running)
        rhos.append(following)
    return rhos[ITERS]


def kernel(
    n_gx,
    n_gy,
    x_hbm,
    solute_hbm,
    exposure_hbm,
    offset_hbm,
    row_hbm,
    live_hbm,
    coupling_hbm,
    cell_hbm,
    evaluation_hbm,
    projection_hbm,
    far_hbm,
    out_ref,
    solute,
    exposure,
    offset,
    row,
    live,
    coupling,
    cell,
    evaluation,
    projection,
    far,
    y,
    z,
    slots,
    whigh,
    wlow,
    source,
    member,
    onehot,
    farhigh,
    farlow,
    kghigh,
    kglow,
    near_cells,
    halo,
    mine,
    part_in,
    plane,
    mid_in,
    whole,
    moments,
    counts,
    scaled,
    expanded,
    unit,
    gram_out,
    gram_in,
    load_sem,
    halo_send,
    halo_recv,
    cell_send,
    cell_recv,
    part_send,
    part_recv,
    mid_send,
    mid_recv,
    whole_send,
    whole_recv,
    gram_send,
    gram_recv,
):
    gx = lax.axis_index("gx")
    gy = lax.axis_index("gy")
    piece = LANES // n_gy

    def peer_y(step):
        return (gx, lax.rem(gy + step, n_gy))

    def peer_x(step):
        return (lax.rem(gx + step, n_gx), gy)

    def beside(index):
        dx, dy = AROUND[index]
        return (lax.rem(gx + dx + n_gx, n_gx), lax.rem(gy + dy + n_gy, n_gy))

    def greet(device):
        pl.semaphore_signal(barrier, inc=1, device_id=device, device_id_type=MESH)

    def each(first, last, act):
        def one(step, carry):
            act(step)
            return carry

        lax.fori_loop(first, last, one, 0)

    loads = [
        pltpu.make_async_copy(there, here, load_sem.at[i])
        for i, (there, here) in enumerate(
            [
                (cell_hbm, cell),
                (offset_hbm, offset),
                (row_hbm, row),
                (live_hbm, live),
                (coupling_hbm, coupling),
                (x_hbm, z.at[0]),
                (x_hbm, y.at[0]),
                (far_hbm, far),
                (evaluation_hbm, evaluation),
                (exposure_hbm, exposure),
                (projection_hbm, projection),
                (solute_hbm, solute),
            ]
        )
    ]
    for load in loads:
        load.start()
    barrier = pltpu.get_barrier_semaphore()
    each(1, n_gy, lambda step: greet(peer_y(step)))
    each(1, n_gx, lambda step: greet(peer_x(step)))
    corners = [i for i, (dx, dy) in enumerate(AROUND) if dx != 0 and dy != 0]
    for i in corners:
        greet(beside(i))

    def bytes_of(ref, sem):
        return pltpu.make_async_copy(ref, ref, sem)

    def halo_copy(k, index):
        return pltpu.make_async_remote_copy(
            src_ref=z.at[k, pl.ds(0, EDGE)],
            dst_ref=halo.at[k, pl.ds((7 - index) * EDGE, EDGE)],
            send_sem=halo_send.at[k, index],
            recv_sem=halo_recv.at[k, 7 - index],
            device_id=beside(index),
            device_id_type=MESH,
        )

    def cell_copy(index):
        return pltpu.make_async_remote_copy(
            src_ref=near_cells.at[8],
            dst_ref=near_cells.at[7 - index],
            send_sem=cell_send.at[index],
            recv_sem=cell_recv.at[7 - index],
            device_id=beside(index),
            device_id_type=MESH,
        )

    def part_copy(k, step):
        return pltpu.make_async_remote_copy(
            src_ref=mine.at[k, lax.rem(gy + step, n_gy)],
            dst_ref=part_in.at[k, step],
            send_sem=part_send.at[k],
            recv_sem=part_recv.at[k],
            device_id=peer_y(step),
            device_id_type=MESH,
        )

    def mid_copy(k, step):
        return pltpu.make_async_remote_copy(
            src_ref=plane.at[k],
            dst_ref=mid_in.at[k, step],
            send_sem=mid_send.at[k],
            recv_sem=mid_recv.at[k],
            device_id=peer_x(step),
            device_id_type=MESH,
        )

    def whole_copy(k, step):
        return pltpu.make_async_remote_copy(
            src_ref=whole.at[k, gy],
            dst_ref=whole.at[k, gy],
            send_sem=whole_send.at[k],
            recv_sem=whole_recv.at[k],
            device_id=peer_y(step),
            device_id_type=MESH,
        )

    def gram_copy(step):
        return pltpu.make_async_remote_copy(
            src_ref=gram_out.at[0],
            dst_ref=gram_in.at[step],
            send_sem=gram_send.at[0],
            recv_sem=gram_recv.at[0],
            device_id=(lax.rem(gx + step // n_gy, n_gx), lax.rem(gy + step % n_gy, n_gy)),
            device_id_type=MESH,
        )

    def prepare(k):
        first = z[k].T[:Q]
        high, rest = split(first)
        middle, last = split(first - high.astype(F32))
        ones = jnp.ones((Q, SPH), BF16)
        stacked = jnp.concatenate([high, middle, last, ones], axis=0)
        parts = dot(stacked, member[...], NT)
        number = parts[3 * Q : 3 * Q + 1]
        parts = parts[:Q] + parts[Q : 2 * Q] + parts[2 * Q : 3 * Q]
        for t in range(TILES):
            columns = slice(t * LANES, (t + 1) * LANES)
            if piece >= Q:
                fold = piece // Q
                mine[k, t // fold, (t % fold) * Q : (t % fold + 1) * Q, :] = parts[:, columns]
                at = piece + t % fold
                mine[k, t // fold, at : at + 1, :] = number[:, columns]
            else:
                per = Q // piece
                for j in range(per):
                    mine[k, t * per + j, :piece, :] = parts[j * piece : (j + 1) * piece, columns]
                    mine[k, t * per + j, piece : piece + 1, :] = number[:, columns]

    def send_halo(k):
        for index in range(8):
            halo_copy(k, index).start()

    def send_part(k):
        each(1, n_gy, functools.partial(lambda k, step: part_copy(k, step).start(), k))

    def pass_on(k):
        bytes_of(part_in.at[k, pl.ds(1, n_gy - 1)], part_recv.at[k]).wait()
        plane[k] = jnp.sum(part_in[k, 1:], axis=0) + mine[k, gy]
        each(1, n_gx, lambda step: mid_copy(k, step).start())

    def spread(k):
        bytes_of(mid_in.at[k, pl.ds(1, n_gx - 1)], mid_recv.at[k]).wait()
        whole[k, gy] = jnp.sum(mid_in[k, 1:], axis=0) + plane[k]
        each(1, n_gy, lambda step: whole_copy(k, step).start())

    index = lax.broadcasted_iota(jnp.int32, (1, H), 1)
    degree = jnp.zeros((1, H), F32)
    for n in range(1, LMAX + 1):
        degree = degree + (index >= n * n).astype(F32)
    scale = jnp.where(index < (LMAX + 1) ** 2, (2.0 * degree + 1.0) / (4.0 * math.pi), 0.0)
    component = lax.broadcasted_iota(jnp.int32, (Q, NC), 0)
    moment_degree = jnp.zeros((Q, NC), F32)
    for n in range(1, 4):
        moment_degree = moment_degree + (component >= n * n).astype(F32)
    moment_scale = (2.0 * moment_degree + 1.0) / (4.0 * math.pi)

    def gathered(k):
        bytes_of(whole.at[k, pl.ds(0, n_gy - 1)], whole_recv.at[k]).wait()
        for t in range(TILES):
            columns = slice(t * LANES, (t + 1) * LANES)
            if piece >= Q:
                fold = piece // Q
                moments[:, columns] = whole[k, t // fold, (t % fold) * Q : (t % fold + 1) * Q, :]
                at = piece + t % fold
                counts[:, columns] = whole[k, t // fold, at : at + 1, :]
            else:
                per = Q // piece
                for j in range(per):
                    moments[j * piece : (j + 1) * piece, columns] = whole[k, t * per + j, :piece, :]
                counts[:, columns] = whole[k, t * per, piece : piece + 1, :]
        value = moment_scale * (moments[...] - counts[...] * expanded[...])
        scaled[...] = value
        high, low = split(value)
        blank = jnp.zeros((H - Q, NC), BF16)
        return jnp.concatenate([high, blank, low, blank], axis=0)

    def distant(both, rows):
        result = dot(kghigh[rows, :], both, NT)
        return result[:, :H] + result[:, H:] + dot(kglow[rows, :], both[:H], NT)

    def expand():
        high, low = split(scaled[...])
        both = dot(jnp.concatenate([high, low], axis=0), farhigh[...])
        expanded[...] = both[:Q] + both[Q:] + dot(high, farlow[...])

    def far_rows(at, first_cells, second_cells):
        cells = jnp.concatenate(
            [
                jnp.broadcast_to(first_cells, (LANES, LANES)).T,
                jnp.broadcast_to(second_cells, (LANES, LANES)).T,
            ],
            axis=0,
        )
        for t in range(TILES):
            numbers = lax.broadcasted_iota(jnp.int32, (SPH, LANES), 1) + t * LANES
            columns = slice(t * LANES, (t + 1) * LANES)
            onehot[:, columns] = (cells == numbers.astype(F32)).astype(F32).astype(BF16)
        rows = slice(at, at + SPH)

        def one(step):
            block = pl.ds(pl.multiple_of(step * SPH, SPH), SPH)
            kghigh[rows, block] = dot(onehot[...], farhigh[block, :], NT).astype(BF16)
            kglow[rows, block] = dot(onehot[...], farlow[block, :], NT).astype(BF16)

        each(0, NC // SPH, one)

    loads[0].wait()
    cell_row = jnp.broadcast_to(cell[...], (LANES, SPH))
    for t in range(TILES):
        cells = lax.broadcasted_iota(jnp.int32, (LANES, SPH), 0) + t * LANES
        member[t * LANES : (t + 1) * LANES, :] = (cell_row == cells).astype(F32).astype(BF16)
    own_cells = cell[...].astype(F32)
    near_cells[8] = jnp.concatenate([own_cells[:, :EDGE], own_cells[:, :EDGE]], axis=1)

    for i in range(1, 5):
        loads[i].wait()
    offsets = offset[...]
    place = jnp.where(
        offsets == 4,
        row[...],
        SPH + jnp.where(offsets > 4, offsets - 1, offsets) * EDGE + row[...],
    )
    alive = jnp.concatenate(
        [jnp.broadcast_to(live[d : d + 1, :], (SLOTS, SPH)) for d in range(ND)], axis=0
    )
    slot = lax.broadcasted_iota(jnp.int32, (NB, SPH), 0) & (SLOTS - 1)
    weights = jnp.where(slot < alive, coupling[...], 0.0)
    blank = jnp.zeros((LANES - 2 * NB, SPH), F32)
    slots[...] = jnp.concatenate([place.astype(F32), weights, blank], axis=0).T

    block_rows = 16

    def weigh(step):
        base = pl.multiple_of(step * block_rows, block_rows)
        held = slots[pl.ds(base, block_rows), :]
        lanes = lax.broadcasted_iota(jnp.int32, (block_rows, LANES), 1).astype(F32)
        for d in range(ND):
            sums = [jnp.zeros((block_rows, LANES), F32) for t in range(SRC // LANES)]
            for s in range(d * SLOTS, (d + 1) * SLOTS):
                where = jnp.broadcast_to(held[:, s : s + 1], (block_rows, LANES))
                value = jnp.broadcast_to(held[:, NB + s : NB + s + 1], (block_rows, LANES))
                for t in range(SRC // LANES):
                    sums[t] = sums[t] + jnp.where(where == lanes + t * LANES, value, 0.0)
            high, low = split(jnp.concatenate(sums, axis=1))
            rows = pl.ds(pl.multiple_of(d * SPH + base, block_rows), block_rows)
            whigh[rows, :] = high
            wlow[rows, :] = low

    each(0, SPH // block_rows, weigh)

    loads[5].wait()
    prepare(0)
    pl.semaphore_wait(barrier, (n_gy - 1) + (n_gx - 1) + len(corners))
    send_halo(0)
    for i in range(8):
        cell_copy(i).start()
    send_part(0)

    loads[7].wait()
    for t in range(TILES):
        rows = slice(t * LANES, (t + 1) * LANES)
        high, low = split(far[rows, :])
        farhigh[rows, :] = high
        farlow[rows, :] = low
    far_rows(0, own_cells[:, :LANES], own_cells[:, LANES:])
    expanded[...] = jnp.zeros_like(expanded)
    for load in loads[8:] + loads[6:7]:
        load.wait()
    evaluation_parts = jnp.concatenate(split(evaluation[...]), axis=1)
    projection_parts = jnp.concatenate(split(projection[...]), axis=1)
    lane = lax.broadcasted_iota(jnp.int32, (1, LANES), 1)

    def product(left, right):
        high, low = split(left)
        both = dot(high, right)
        return both[:, :H] + both[:, H:] + dot(low, right[:, :H])

    def neighbour_cells(pair):
        return jnp.where(lane < EDGE, near_cells[2 * pair], near_cells[2 * pair + 1])

    def put(rows, value):
        high, low = split(value)
        source[rows, :H] = high
        source[rows, H:] = low

    def iterate(k, carry):
        @pl.when(k == 1)
        def _():
            for i in range(8):
                cell_copy(i).wait_recv()
            far_rows(SPH, neighbour_cells(0), neighbour_cells(1))

        @pl.when(k > 0)
        def _():
            spread(k - 1)

        @pl.when(k == 1)
        def _():
            far_rows(2 * SPH, neighbour_cells(2), neighbour_cells(3))

        pass_on(k)

        for i in range(8):
            halo_copy(k, i).wait_recv()

        @pl.when(k == 0)
        def _():
            put(slice(0, SPH), y[0])
            put(slice(SPH, SRC), halo[0])

        @pl.when(k > 0)
        def _():
            taken = distant(gathered(k - 1), slice(0, SRC))
            own = z[k] - taken[:SPH]
            y[k] = own
            put(slice(0, SPH), own)
            put(slice(SPH, SRC), halo[k] - taken[SPH:])

        potential = jnp.zeros((SPH, H), F32)
        for d in range(ND):
            rows = slice(d * SPH, (d + 1) * SPH)
            both = dot(whigh[rows, :], source[...])
            sums = both[:, :H] + both[:, H:] + dot(wlow[rows, :], source[:, :H])
            potential = potential + product(sums, evaluation_parts[d * H : (d + 1) * H])
        nearby = product(potential * exposure[...], projection_parts)
        z[k + 1] = scale * (solute[...] - nearby)

        @pl.when(k < ITERS - 1)
        def _():
            send_halo(k + 1)
            prepare(k + 1)
            send_part(k + 1)

        @pl.when(k > 0)
        def _():
            expand()

        return carry

    lax.fori_loop(0, ITERS, iterate, 0)

    spread(ITERS - 1)
    pairs = [(a, b) for a in range(ITERS) for b in range(a + 1)]
    early = [y[k + 1] - y[k] for k in range(ITERS - 1)]
    height = jnp.abs(early[0])
    for change in early[1:]:
        height = jnp.maximum(height, jnp.abs(change))
    top = largest(height)
    top = jnp.where(top > 0.0, top, 1.0)
    inverse = 1.0 / top
    for k in range(ITERS - 1):
        unit[k] = early[k] * inverse
    line = jnp.zeros((1, LANES), F32)
    for i, (a, b) in enumerate(pairs):
        if a < ITERS - 1:
            line = line + jnp.where(lane == i, total(unit[a] * unit[b]), 0.0)

    last = z[ITERS] - distant(gathered(ITERS - 1), slice(0, SPH))
    y[ITERS] = last
    change = last - y[ITERS - 1]
    most = jnp.maximum(top, largest(jnp.abs(change)))
    ratio = top / most
    change = change * (1.0 / most)
    line = line * (ratio * ratio)
    for i, (a, b) in enumerate(pairs):
        if a == ITERS - 1:
            sums = total(change * change) if b == a else total(change * unit[b]) * ratio
            line = line + jnp.where(lane == i, sums, 0.0)
    line = jnp.where(lane == len(pairs), most, line)
    gram_out[0] = line
    gram_in[0] = line
    everyone = n_gx * n_gy
    each(1, everyone, lambda step: gram_copy(step).start())
    bytes_of(gram_in.at[pl.ds(1, everyone - 1)], gram_recv.at[0]).wait()
    lines = gram_in[...].reshape(everyone, LANES)
    tops = lines[:, len(pairs) : len(pairs) + 1]
    ratio = tops / jnp.max(tops, axis=0, keepdims=True)
    line = jnp.sum(lines * (ratio * ratio), axis=0, keepdims=True)

    gram = [[None] * ITERS for a in range(ITERS)]
    for i, (a, b) in enumerate(pairs):
        gram[a][b] = line[:, i : i + 1]
    rho = mixed_coefficients(gram)
    mixed = rho[1] * y[1]
    for k in range(2, ITERS + 1):
        mixed = mixed + rho[k] * y[k]
    out_ref[...] = mixed

    def sent(k):
        for i in range(8):
            halo_copy(k, i).wait_send()
        peers = pl.ds(0, n_gy - 1)
        bytes_of(mine.at[k, peers], part_send.at[k]).wait()
        bytes_of(mid_in.at[k, pl.ds(1, n_gx - 1)], mid_send.at[k]).wait()
        bytes_of(whole.at[k, peers], whole_send.at[k]).wait()

    each(0, ITERS, sent)
    for i in range(8):
        cell_copy(i).wait_send()
    bytes_of(gram_in.at[pl.ds(1, everyone - 1)], gram_send.at[0]).wait()


def per_device(
    n_gx,
    n_gy,
    start_charges,
    solute_field,
    exposure,
    owner_offset,
    owner_row,
    live_slots,
    coupling,
    cell_index,
    evaluation,
    projection,
    far_kernel,
):
    hbm = pl.BlockSpec(memory_space=pl.ANY)
    piece = LANES // n_gy
    rows = piece + max(1, piece // Q)
    dma = pltpu.SemaphoreType.DMA

    def held(*shape, dtype=F32):
        return pltpu.VMEM(shape, dtype)

    return pl.pallas_call(
        functools.partial(kernel, n_gx, n_gy),
        out_shape=jax.ShapeDtypeStruct((SPH, H), F32),
        in_specs=[hbm] * 11,
        out_specs=pl.BlockSpec(memory_space=pltpu.VMEM),
        scratch_shapes=[
            held(SPH, H),
            held(SPH, H),
            held(NB, SPH, dtype=jnp.int32),
            held(NB, SPH, dtype=jnp.int32),
            held(ND, SPH, dtype=jnp.int32),
            held(NB, SPH),
            held(1, SPH, dtype=jnp.int32),
            held(ND * H, H),
            held(H, H),
            held(NC, NC),
            held(ITERS + 1, SPH, H),
            held(ITERS + 1, SPH, H),
            held(SPH, LANES),
            held(ND * SPH, SRC, dtype=BF16),
            held(ND * SPH, SRC, dtype=BF16),
            held(SRC, 2 * H, dtype=BF16),
            held(NC, SPH, dtype=BF16),
            held(SPH, NC, dtype=BF16),
            held(NC, NC, dtype=BF16),
            held(NC, NC, dtype=BF16),
            held(SRC, NC, dtype=BF16),
            held(SRC, NC, dtype=BF16),
            held(9, 1, LANES),
            held(ITERS, 8 * EDGE, H),
            held(ITERS, n_gy, rows, LANES),
            held(ITERS, n_gy, rows, LANES),
            held(ITERS, rows, LANES),
            held(ITERS, n_gx, rows, LANES),
            held(ITERS, n_gy, rows, LANES),
            held(Q, NC),
            held(1, NC),
            held(Q, NC),
            held(Q, NC),
            held(ITERS - 1, SPH, H),
            held(1, 1, LANES),
            held(n_gx * n_gy, 1, LANES),
            dma((12,)),
            dma((ITERS, 8)),
            dma((ITERS, 8)),
            dma((8,)),
            dma((8,)),
            dma((ITERS,)),
            dma((ITERS,)),
            dma((ITERS,)),
            dma((ITERS,)),
            dma((ITERS,)),
            dma((ITERS,)),
            dma((1,)),
            dma((1,)),
        ],
        compiler_params=pltpu.CompilerParams(
            collective_id=0, has_side_effects=True, vmem_limit_bytes=60 * 1024 * 1024
        ),
        name="screening",
    )(
        start_charges,
        solute_field,
        exposure,
        owner_offset.T,
        owner_row.T,
        live_slots.T,
        coupling.T,
        cell_index.reshape(1, SPH),
        evaluation,
        projection,
        far_kernel,
    )


def solution(mesh):
    placed = (
        P(("gx", "gy"), None),
        P(("gx", "gy"), None),
        P(("gx", "gy"), None),
        P(("gx", "gy"), None),
        P(("gx", "gy"), None),
        P(("gx", "gy"), None),
        P(("gx", "gy"), None),
        P(("gx", "gy")),
        P(),
        P(),
        P(),
    )
    return jax.shard_map(
        functools.partial(per_device, mesh.shape["gx"], mesh.shape["gy"]),
        mesh=mesh,
        in_specs=placed,
        out_specs=P(("gx", "gy"), None),
        check_vma=False,
    )
```

```python
import functools
import math

import jax
import jax.numpy as jnp
from jax import lax
from jax.experimental import pallas as pl
from jax.experimental.pallas import tpu as pltpu
from jax.sharding import PartitionSpec as P

MESH = pl.DeviceIdType.MESH
F32 = jnp.float32
BF16 = jnp.bfloat16

LMAX = 10
H = 128
Q = 16
ND = 4
SLOTS = 8
NB = 32
EDGE = 64
ITERS = 4
SPH = 256
NC = 1024
SRC = SPH + 8 * EDGE
LANES = 128
TILES = NC // LANES
AROUND = [(dx, dy) for dx in (-1, 0, 1) for dy in (-1, 0, 1) if (dx, dy) != (0, 0)]
FARTHEST = (0, 2, 5, 7, 1, 6, 3, 4)
NN = (((1,), (0,)), ((), ()))
NT = (((1,), (1,)), ((), ()))


def spd_mixing(margins):
    order = len(margins)
    diagonal_sum = margins[0][0]
    for a in range(1, order):
        diagonal_sum = diagonal_sum + margins[a][a]
    damping = 0.01 * diagonal_sum / order
    triangle = [[None] * order for a in range(order)]
    for a in range(order):
        for b in range(a + 1):
            running = margins[a][b] + (damping if a == b else 0.0)
            for c in range(b):
                running = running - triangle[a][c] * triangle[b][c]
            if a == b:
                triangle[a][a] = jnp.sqrt(running)
            else:
                triangle[a][b] = running / triangle[b][b]
    forward = []
    for a in range(order):
        running = jnp.ones_like(diagonal_sum)
        for c in range(a):
            running = running - triangle[a][c] * forward[c]
        forward.append(running / triangle[a][a])
    backward = [None] * order
    for a in reversed(range(order)):
        running = forward[a]
        for c in range(a + 1, order):
            running = running - triangle[c][a] * backward[c]
        backward[a] = running / triangle[a][a]
    weight_sum = backward[0]
    for a in range(1, order):
        weight_sum = weight_sum + backward[a]
    return [value / weight_sum for value in backward]


def split(value):
    high = value.astype(BF16)
    return high, (value - high.astype(F32)).astype(BF16)


def dot(a, b, dims=NN):
    return lax.dot_general(a, b, dims, preferred_element_type=F32)


def total(value):
    rows = jnp.sum(value.reshape(-1, 8, LANES), axis=0)
    return jnp.sum(jnp.sum(rows, axis=0, keepdims=True), axis=1, keepdims=True)


def largest(value):
    rows = jnp.max(value.reshape(-1, 8, LANES), axis=0)
    return jnp.max(jnp.max(rows, axis=0, keepdims=True), axis=1, keepdims=True)


def mixed_coefficients(gram):
    zero = jnp.zeros_like(gram[0][0])
    one = jnp.ones_like(zero)
    rhos = [[one] + [zero] * ITERS]
    margins = []
    for t in range(ITERS):
        new = rhos[t]
        image = []
        for l in range(ITERS):
            running = None
            for k in range(t + 1):
                term = new[k] * gram[max(k, l)][min(k, l)]
                running = term if running is None else running + term
            image.append(running)
        row = []
        for a in range(t + 1):
            running = None
            for l in range(a + 1):
                term = rhos[a][l] * image[l]
                running = term if running is None else running + term
            row.append(running)
        margins.append(row)
        full = [[margins[max(a, b)][min(a, b)] for b in range(t + 1)] for a in range(t + 1)]
        mixing = spd_mixing(full)
        following = [zero]
        for k in range(ITERS):
            running = zero
            for a in range(t + 1):
                if k <= a:
                    running = running + mixing[a] * rhos[a][k]
            following.append(running)
        rhos.append(following)
    return rhos[ITERS]


def kernel(
    n_gx,
    n_gy,
    x_hbm,
    solute_hbm,
    exposure_hbm,
    offset_hbm,
    row_hbm,
    live_hbm,
    coupling_hbm,
    cell_hbm,
    evaluation_hbm,
    projection_hbm,
    far_hbm,
    out_ref,
    solute,
    exposure,
    offset,
    row,
    live,
    coupling,
    cell,
    evaluation,
    projection,
    far,
    y,
    z,
    slots,
    whigh,
    wlow,
    source,
    member,
    onehot,
    farhigh,
    farlow,
    kghigh,
    kglow,
    near_cells,
    halo,
    mine,
    part_in,
    plane,
    mid_in,
    whole,
    moments,
    counts,
    scaled,
    expanded,
    unit,
    pair_out,
    pair_in,
    gram_out,
    gram_in,
    load_sem,
    halo_send,
    halo_recv,
    cell_send,
    cell_recv,
    part_send,
    part_recv,
    mid_send,
    mid_recv,
    whole_send,
    whole_recv,
    gram_send,
    gram_recv,
):
    gx = lax.axis_index("gx")
    gy = lax.axis_index("gy")
    piece = LANES // n_gy

    def peer_y(step):
        return (gx, lax.rem(gy + step, n_gy))

    def peer_x(step):
        return (lax.rem(gx + step, n_gx), gy)

    def beside(index):
        dx, dy = AROUND[index]
        return (lax.rem(gx + dx + n_gx, n_gx), lax.rem(gy + dy + n_gy, n_gy))

    def greet(device):
        pl.semaphore_signal(barrier, inc=1, device_id=device, device_id_type=MESH)

    def each(first, last, act):
        def one(step, carry):
            act(step)
            return carry

        lax.fori_loop(first, last, one, 0)

    loads = [
        pltpu.make_async_copy(there, here, load_sem.at[i])
        for i, (there, here) in enumerate(
            [
                (cell_hbm, cell),
                (offset_hbm, offset),
                (row_hbm, row),
                (live_hbm, live),
                (coupling_hbm, coupling),
                (x_hbm, z.at[0]),
                (x_hbm, y.at[0]),
                (far_hbm, far),
                (evaluation_hbm, evaluation),
                (exposure_hbm, exposure),
                (projection_hbm, projection),
                (solute_hbm, solute),
            ]
        )
    ]
    for load in loads:
        load.start()
    barrier = pltpu.get_barrier_semaphore()
    each(1, n_gy, lambda step: greet(peer_y(step)))
    each(1, n_gx, lambda step: greet(peer_x(step)))
    corners = [i for i, (dx, dy) in enumerate(AROUND) if dx != 0 and dy != 0]
    for i in corners:
        greet(beside(i))

    def bytes_of(ref, sem):
        return pltpu.make_async_copy(ref, ref, sem)

    def halo_copy(k, index):
        return pltpu.make_async_remote_copy(
            src_ref=z.at[k, pl.ds(0, EDGE)],
            dst_ref=halo.at[k, pl.ds((7 - index) * EDGE, EDGE)],
            send_sem=halo_send.at[k, index],
            recv_sem=halo_recv.at[k, 7 - index],
            device_id=beside(index),
            device_id_type=MESH,
        )

    def cell_copy(index):
        return pltpu.make_async_remote_copy(
            src_ref=near_cells.at[8],
            dst_ref=near_cells.at[7 - index],
            send_sem=cell_send.at[index],
            recv_sem=cell_recv.at[7 - index],
            device_id=beside(index),
            device_id_type=MESH,
        )

    def part_copy(k, step):
        return pltpu.make_async_remote_copy(
            src_ref=mine.at[k, lax.rem(gy + step, n_gy)],
            dst_ref=part_in.at[k, step],
            send_sem=part_send.at[k],
            recv_sem=part_recv.at[k],
            device_id=peer_y(step),
            device_id_type=MESH,
        )

    def mid_copy(k, step):
        return pltpu.make_async_remote_copy(
            src_ref=plane.at[k],
            dst_ref=mid_in.at[k, step],
            send_sem=mid_send.at[k],
            recv_sem=mid_recv.at[k],
            device_id=peer_x(step),
            device_id_type=MESH,
        )

    def whole_copy(k, step):
        return pltpu.make_async_remote_copy(
            src_ref=whole.at[k, gy],
            dst_ref=whole.at[k, gy],
            send_sem=whole_send.at[k],
            recv_sem=whole_recv.at[k],
            device_id=peer_y(step),
            device_id_type=MESH,
        )

    def gram_copy(step):
        return pltpu.make_async_remote_copy(
            src_ref=gram_out.at[0],
            dst_ref=gram_in.at[step],
            send_sem=gram_send.at[0],
            recv_sem=gram_recv.at[0],
            device_id=(
                lax.rem(gx + step // (n_gy // 2), n_gx),
                lax.rem(gy + 2 * (step % (n_gy // 2)), n_gy),
            ),
            device_id_type=MESH,
        )

    def pair_copy():
        return pltpu.make_async_remote_copy(
            src_ref=pair_out.at[0],
            dst_ref=pair_in.at[0],
            send_sem=gram_send.at[1],
            recv_sem=gram_recv.at[1],
            device_id=(gx, gy + 1 - 2 * lax.rem(gy, 2)),
            device_id_type=MESH,
        )

    def sent(k):
        for i in range(8):
            halo_copy(k, i).wait_send()
        peers = pl.ds(0, n_gy - 1)
        bytes_of(mine.at[k, peers], part_send.at[k]).wait()
        bytes_of(mid_in.at[k, pl.ds(1, n_gx - 1)], mid_send.at[k]).wait()
        bytes_of(whole.at[k, peers], whole_send.at[k]).wait()

    def prepare(k):
        first = z[k].T[:Q]
        high, rest = split(first)
        middle, last = split(first - high.astype(F32))
        ones = jnp.ones((Q, SPH), BF16)
        stacked = jnp.concatenate([high, middle, last, ones], axis=0)
        parts = dot(stacked, member[...], NT)
        number = parts[3 * Q : 3 * Q + 1]
        parts = parts[:Q] + parts[Q : 2 * Q] + parts[2 * Q : 3 * Q]
        for t in range(TILES):
            columns = slice(t * LANES, (t + 1) * LANES)
            if piece >= Q:
                fold = piece // Q
                mine[k, t // fold, (t % fold) * Q : (t % fold + 1) * Q, :] = parts[:, columns]
                at = piece + t % fold
                mine[k, t // fold, at : at + 1, :] = number[:, columns]
            else:
                per = Q // piece
                for j in range(per):
                    mine[k, t * per + j, :piece, :] = parts[j * piece : (j + 1) * piece, columns]
                    mine[k, t * per + j, piece : piece + 1, :] = number[:, columns]

    def send_halo(k):
        for index in FARTHEST:
            halo_copy(k, index).start()

    def send_part(k):
        each(1, n_gy, functools.partial(lambda k, step: part_copy(k, step).start(), k))

    def pass_on(k):
        bytes_of(part_in.at[k, pl.ds(1, n_gy - 1)], part_recv.at[k]).wait()
        plane[k] = jnp.sum(part_in[k, 1:], axis=0) + mine[k, gy]
        each(1, n_gx, lambda step: mid_copy(k, step).start())

    def spread(k):
        bytes_of(mid_in.at[k, pl.ds(1, n_gx - 1)], mid_recv.at[k]).wait()
        whole[k, gy] = jnp.sum(mid_in[k, 1:], axis=0) + plane[k]
        each(1, n_gy, lambda step: whole_copy(k, step).start())

    index = lax.broadcasted_iota(jnp.int32, (1, H), 1)
    degree = jnp.zeros((1, H), F32)
    for n in range(1, LMAX + 1):
        degree = degree + (index >= n * n).astype(F32)
    scale = jnp.where(index < (LMAX + 1) ** 2, (2.0 * degree + 1.0) / (4.0 * math.pi), 0.0)
    component = lax.broadcasted_iota(jnp.int32, (Q, NC), 0)
    moment_degree = jnp.zeros((Q, NC), F32)
    for n in range(1, 4):
        moment_degree = moment_degree + (component >= n * n).astype(F32)
    moment_scale = (2.0 * moment_degree + 1.0) / (4.0 * math.pi)

    def gathered(k):
        bytes_of(whole.at[k, pl.ds(0, n_gy - 1)], whole_recv.at[k]).wait()
        for t in range(TILES):
            columns = slice(t * LANES, (t + 1) * LANES)
            if piece >= Q:
                fold = piece // Q
                moments[:, columns] = whole[k, t // fold, (t % fold) * Q : (t % fold + 1) * Q, :]
                at = piece + t % fold
                counts[:, columns] = whole[k, t // fold, at : at + 1, :]
            else:
                per = Q // piece
                for j in range(per):
                    moments[j * piece : (j + 1) * piece, columns] = whole[k, t * per + j, :piece, :]
                counts[:, columns] = whole[k, t * per, piece : piece + 1, :]
        value = moment_scale * (moments[...] - counts[...] * expanded[...])
        scaled[...] = value
        high, low = split(value)
        blank = jnp.zeros((H - Q, NC), BF16)
        return jnp.concatenate([high, blank, low, blank], axis=0)

    def distant(both, rows):
        result = dot(kghigh[rows, :], both, NT)
        return result[:, :H] + result[:, H:] + dot(kglow[rows, :], both[:H], NT)

    def expand():
        high, low = split(scaled[...])
        both = dot(jnp.concatenate([high, low], axis=0), farhigh[...])
        expanded[...] = both[:Q] + both[Q:] + dot(high, farlow[...])

    def far_rows(at, first_cells, second_cells):
        cells = jnp.concatenate(
            [
                jnp.broadcast_to(first_cells, (LANES, LANES)).T,
                jnp.broadcast_to(second_cells, (LANES, LANES)).T,
            ],
            axis=0,
        )
        for t in range(TILES):
            numbers = lax.broadcasted_iota(jnp.int32, (SPH, LANES), 1) + t * LANES
            columns = slice(t * LANES, (t + 1) * LANES)
            onehot[:, columns] = (cells == numbers.astype(F32)).astype(F32).astype(BF16)
        rows = slice(at, at + SPH)

        def one(step):
            block = pl.ds(pl.multiple_of(step * SPH, SPH), SPH)
            kghigh[rows, block] = dot(onehot[...], farhigh[block, :], NT).astype(BF16)
            kglow[rows, block] = dot(onehot[...], farlow[block, :], NT).astype(BF16)

        each(0, NC // SPH, one)

    loads[0].wait()
    cell_row = jnp.broadcast_to(cell[...], (LANES, SPH))
    for t in range(TILES):
        cells = lax.broadcasted_iota(jnp.int32, (LANES, SPH), 0) + t * LANES
        member[t * LANES : (t + 1) * LANES, :] = (cell_row == cells).astype(F32).astype(BF16)
    own_cells = cell[...].astype(F32)
    near_cells[8] = jnp.concatenate([own_cells[:, :EDGE], own_cells[:, :EDGE]], axis=1)

    for i in range(1, 5):
        loads[i].wait()
    offsets = offset[...]
    place = jnp.where(
        offsets == 4,
        row[...],
        SPH + jnp.where(offsets > 4, offsets - 1, offsets) * EDGE + row[...],
    )
    alive = jnp.concatenate(
        [jnp.broadcast_to(live[d : d + 1, :], (SLOTS, SPH)) for d in range(ND)], axis=0
    )
    slot = lax.broadcasted_iota(jnp.int32, (NB, SPH), 0) & (SLOTS - 1)
    weights = jnp.where(slot < alive, coupling[...], 0.0)
    blank = jnp.zeros((LANES - 2 * NB, SPH), F32)
    slots[...] = jnp.concatenate([place.astype(F32), weights, blank], axis=0).T

    block_rows = 16

    def weigh(step):
        base = pl.multiple_of(step * block_rows, block_rows)
        held = slots[pl.ds(base, block_rows), :]
        lanes = lax.broadcasted_iota(jnp.int32, (block_rows, LANES), 1).astype(F32)
        for d in range(ND):
            sums = [jnp.zeros((block_rows, LANES), F32) for t in range(SRC // LANES)]
            for s in range(d * SLOTS, (d + 1) * SLOTS):
                where = jnp.broadcast_to(held[:, s : s + 1], (block_rows, LANES))
                value = jnp.broadcast_to(held[:, NB + s : NB + s + 1], (block_rows, LANES))
                for t in range(SRC // LANES):
                    sums[t] = sums[t] + jnp.where(where == lanes + t * LANES, value, 0.0)
            high, low = split(jnp.concatenate(sums, axis=1))
            rows = pl.ds(pl.multiple_of(d * SPH + base, block_rows), block_rows)
            whigh[rows, :] = high
            wlow[rows, :] = low


    loads[5].wait()
    prepare(0)
    pl.semaphore_wait(barrier, (n_gy - 1) + (n_gx - 1) + len(corners))
    send_part(0)
    send_halo(0)
    for i in range(8):
        cell_copy(i).start()
    each(0, SPH // block_rows, weigh)

    loads[7].wait()
    for t in range(TILES):
        rows = slice(t * LANES, (t + 1) * LANES)
        high, low = split(far[rows, :])
        farhigh[rows, :] = high
        farlow[rows, :] = low
    expanded[...] = jnp.zeros_like(expanded)
    for load in loads[8:] + loads[6:7]:
        load.wait()
    evaluation_parts = jnp.concatenate(split(evaluation[...]), axis=1)
    projection_parts = jnp.concatenate(split(projection[...]), axis=1)
    lane = lax.broadcasted_iota(jnp.int32, (1, LANES), 1)

    def product(left, right):
        high, low = split(left)
        both = dot(high, right)
        return both[:, :H] + both[:, H:] + dot(low, right[:, :H])

    def neighbour_cells(pair):
        return jnp.where(lane < EDGE, near_cells[2 * pair], near_cells[2 * pair + 1])

    def put(rows, value):
        high, low = split(value)
        source[rows, :H] = high
        source[rows, H:] = low

    def iterate(k, carry):
        @pl.when(k == 1)
        def _():
            for i in range(8):
                cell_copy(i).wait_recv()
            far_rows(SPH, neighbour_cells(0), neighbour_cells(1))

        @pl.when(k > 0)
        def _():
            spread(k - 1)

        @pl.when(k > 1)
        def _():
            expand()

        @pl.when(k == 1)
        def _():
            far_rows(2 * SPH, neighbour_cells(2), neighbour_cells(3))

        pass_on(k)

        @pl.when(k == 1)
        def _():
            cells = cell[...].astype(F32)
            far_rows(0, cells[:, :LANES], cells[:, LANES:])

        for i in range(8):
            halo_copy(k, i).wait_recv()

        @pl.when(k == 0)
        def _():
            put(slice(0, SPH), y[0])
            put(slice(SPH, SRC), halo[0])

        @pl.when(k > 0)
        def _():
            taken = distant(gathered(k - 1), slice(0, SRC))
            own = z[k] - taken[:SPH]
            y[k] = own
            put(slice(0, SPH), own)
            put(slice(SPH, SRC), halo[k] - taken[SPH:])

        potential = jnp.zeros((SPH, H), F32)
        for pair in range(ND // 2):
            sums = []
            for d in (2 * pair, 2 * pair + 1):
                rows = slice(d * SPH, (d + 1) * SPH)
                both = dot(whigh[rows, :], source[...])
                low = dot(wlow[rows, :], source[:, :H])
                sums.append(both[:, :H] + both[:, H:] + low)
            rows = slice(2 * pair * H, 2 * (pair + 1) * H)
            potential = potential + product(
                jnp.concatenate(sums, axis=1), evaluation_parts[rows]
            )
        nearby = product(potential * exposure[...], projection_parts)
        z[k + 1] = scale * (solute[...] - nearby)

        @pl.when(k < ITERS - 1)
        def _():
            @pl.when(k == 1)
            def _():
                send_halo(k + 1)

            prepare(k + 1)
            send_part(k + 1)

            @pl.when(k != 1)
            def _():
                send_halo(k + 1)

        return carry

    lax.fori_loop(0, ITERS, iterate, 0)

    spread(ITERS - 1)
    expand()
    pairs = [(a, b) for a in range(ITERS) for b in range(a + 1)]
    early = [y[k + 1] - y[k] for k in range(ITERS - 1)]
    height = jnp.abs(early[0])
    for change in early[1:]:
        height = jnp.maximum(height, jnp.abs(change))
    top = largest(height)
    top = jnp.where(top > 0.0, top, 1.0)
    inverse = 1.0 / top
    for k in range(ITERS - 1):
        unit[k] = early[k] * inverse
    line = jnp.zeros((1, LANES), F32)
    for i, (a, b) in enumerate(pairs):
        if a < ITERS - 1:
            line = line + jnp.where(lane == i, total(unit[a] * unit[b]), 0.0)

    last = z[ITERS] - distant(gathered(ITERS - 1), slice(0, SPH))
    y[ITERS] = last
    change = last - y[ITERS - 1]
    most = jnp.maximum(top, largest(jnp.abs(change)))
    ratio = top / most
    change = change * (1.0 / most)
    line = line * (ratio * ratio)
    for i, (a, b) in enumerate(pairs):
        if a == ITERS - 1:
            sums = total(change * change) if b == a else total(change * unit[b]) * ratio
            line = line + jnp.where(lane == i, sums, 0.0)
    line = jnp.where(lane == len(pairs), most, line)
    def merged(lines):
        tops = lines[:, len(pairs) : len(pairs) + 1]
        most = jnp.max(tops, axis=0, keepdims=True)
        ratio = tops / most
        sums = jnp.sum(lines * (ratio * ratio), axis=0, keepdims=True)
        return jnp.where(lane == len(pairs), most, sums)

    pair_out[0] = line
    pair_copy().start()
    pair_copy().wait_recv()
    line = merged(jnp.concatenate([line, pair_in[0]], axis=0))
    gram_out[0] = line
    gram_in[0] = line
    chips = n_gx * n_gy // 2
    each(1, chips, lambda step: gram_copy(step).start())
    each(0, ITERS, sent)
    for i in range(8):
        cell_copy(i).wait_send()
    pair_copy().wait_send()
    bytes_of(gram_in.at[pl.ds(1, chips - 1)], gram_recv.at[0]).wait()
    line = merged(gram_in[...].reshape(chips, LANES))

    gram = [[None] * ITERS for a in range(ITERS)]
    for i, (a, b) in enumerate(pairs):
        gram[a][b] = line[:, i : i + 1]
    rho = mixed_coefficients(gram)
    mixed = rho[1] * y[1]
    for k in range(2, ITERS + 1):
        mixed = mixed + rho[k] * y[k]
    out_ref[...] = mixed

    bytes_of(gram_in.at[pl.ds(1, chips - 1)], gram_send.at[0]).wait()


def per_device(
    n_gx,
    n_gy,
    start_charges,
    solute_field,
    exposure,
    owner_offset,
    owner_row,
    live_slots,
    coupling,
    cell_index,
    evaluation,
    projection,
    far_kernel,
):
    hbm = pl.BlockSpec(memory_space=pl.ANY)
    piece = LANES // n_gy
    rows = piece + max(1, piece // Q)
    dma = pltpu.SemaphoreType.DMA

    def held(*shape, dtype=F32):
        return pltpu.VMEM(shape, dtype)

    return pl.pallas_call(
        functools.partial(kernel, n_gx, n_gy),
        out_shape=jax.ShapeDtypeStruct((SPH, H), F32),
        in_specs=[hbm] * 11,
        out_specs=pl.BlockSpec(memory_space=pltpu.VMEM),
        scratch_shapes=[
            held(SPH, H),
            held(SPH, H),
            held(NB, SPH, dtype=jnp.int32),
            held(NB, SPH, dtype=jnp.int32),
            held(ND, SPH, dtype=jnp.int32),
            held(NB, SPH),
            held(1, SPH, dtype=jnp.int32),
            held(ND * H, H),
            held(H, H),
            held(NC, NC),
            held(ITERS + 1, SPH, H),
            held(ITERS + 1, SPH, H),
            held(SPH, LANES),
            held(ND * SPH, SRC, dtype=BF16),
            held(ND * SPH, SRC, dtype=BF16),
            held(SRC, 2 * H, dtype=BF16),
            held(NC, SPH, dtype=BF16),
            held(SPH, NC, dtype=BF16),
            held(NC, NC, dtype=BF16),
            held(NC, NC, dtype=BF16),
            held(SRC, NC, dtype=BF16),
            held(SRC, NC, dtype=BF16),
            held(9, 1, LANES),
            held(ITERS, 8 * EDGE, H),
            held(ITERS, n_gy, rows, LANES),
            held(ITERS, n_gy, rows, LANES),
            held(ITERS, rows, LANES),
            held(ITERS, n_gx, rows, LANES),
            held(ITERS, n_gy, rows, LANES),
            held(Q, NC),
            held(1, NC),
            held(Q, NC),
            held(Q, NC),
            held(ITERS - 1, SPH, H),
            held(1, 1, LANES),
            held(1, 1, LANES),
            held(1, 1, LANES),
            held(n_gx * n_gy // 2, 1, LANES),
            dma((12,)),
            dma((ITERS, 8)),
            dma((ITERS, 8)),
            dma((8,)),
            dma((8,)),
            dma((ITERS,)),
            dma((ITERS,)),
            dma((ITERS,)),
            dma((ITERS,)),
            dma((ITERS,)),
            dma((ITERS,)),
            dma((2,)),
            dma((2,)),
        ],
        compiler_params=pltpu.CompilerParams(
            collective_id=0, has_side_effects=True, vmem_limit_bytes=60 * 1024 * 1024
        ),
        name="screening",
    )(
        start_charges,
        solute_field,
        exposure,
        owner_offset.T,
        owner_row.T,
        live_slots.T,
        coupling.T,
        cell_index.reshape(1, SPH),
        evaluation,
        projection,
        far_kernel,
    )


def solution(mesh):
    placed = (
        P(("gx", "gy"), None),
        P(("gx", "gy"), None),
        P(("gx", "gy"), None),
        P(("gx", "gy"), None),
        P(("gx", "gy"), None),
        P(("gx", "gy"), None),
        P(("gx", "gy"), None),
        P(("gx", "gy")),
        P(),
        P(),
        P(),
    )
    return jax.shard_map(
        functools.partial(per_device, mesh.shape["gx"], mesh.shape["gy"]),
        mesh=mesh,
        in_specs=placed,
        out_specs=P(("gx", "gy"), None),
        check_vma=False,
    )
```

```python
import functools
import math

import jax
import jax.numpy as jnp
from jax import lax
from jax.experimental import pallas as pl
from jax.experimental.pallas import tpu as pltpu
from jax.sharding import PartitionSpec as P

MESH = pl.DeviceIdType.MESH
F32 = jnp.float32
BF16 = jnp.bfloat16

LMAX = 10
H = 128
Q = 16
ND = 4
SLOTS = 8
NB = 32
EDGE = 64
ITERS = 4
SPH = 256
NC = 1024
SRC = SPH + 8 * EDGE
LANES = 128
TILES = NC // LANES
AROUND = [(dx, dy) for dx in (-1, 0, 1) for dy in (-1, 0, 1) if (dx, dy) != (0, 0)]
FARTHEST = (0, 2, 5, 7, 1, 6, 3, 4)
NN = (((1,), (0,)), ((), ()))
NT = (((1,), (1,)), ((), ()))


def spd_mixing(margins):
    order = len(margins)
    diagonal_sum = margins[0][0]
    for a in range(1, order):
        diagonal_sum = diagonal_sum + margins[a][a]
    damping = 0.01 * diagonal_sum / order
    triangle = [[None] * order for a in range(order)]
    for a in range(order):
        for b in range(a + 1):
            running = margins[a][b] + (damping if a == b else 0.0)
            for c in range(b):
                running = running - triangle[a][c] * triangle[b][c]
            if a == b:
                triangle[a][a] = jnp.sqrt(running)
            else:
                triangle[a][b] = running / triangle[b][b]
    forward = []
    for a in range(order):
        running = jnp.ones_like(diagonal_sum)
        for c in range(a):
            running = running - triangle[a][c] * forward[c]
        forward.append(running / triangle[a][a])
    backward = [None] * order
    for a in reversed(range(order)):
        running = forward[a]
        for c in range(a + 1, order):
            running = running - triangle[c][a] * backward[c]
        backward[a] = running / triangle[a][a]
    weight_sum = backward[0]
    for a in range(1, order):
        weight_sum = weight_sum + backward[a]
    return [value / weight_sum for value in backward]


def split(value):
    high = value.astype(BF16)
    return high, (value - high.astype(F32)).astype(BF16)


def dot(a, b, dims=NN):
    return lax.dot_general(a, b, dims, preferred_element_type=F32)


def total(value):
    rows = jnp.sum(value.reshape(-1, 8, LANES), axis=0)
    return jnp.sum(jnp.sum(rows, axis=0, keepdims=True), axis=1, keepdims=True)


def largest(value):
    rows = jnp.max(value.reshape(-1, 8, LANES), axis=0)
    return jnp.max(jnp.max(rows, axis=0, keepdims=True), axis=1, keepdims=True)


def mixed_coefficients(gram):
    zero = jnp.zeros_like(gram[0][0])
    one = jnp.ones_like(zero)
    rhos = [[one] + [zero] * ITERS]
    margins = []
    for t in range(ITERS):
        new = rhos[t]
        image = []
        for l in range(ITERS):
            running = None
            for k in range(t + 1):
                term = new[k] * gram[max(k, l)][min(k, l)]
                running = term if running is None else running + term
            image.append(running)
        row = []
        for a in range(t + 1):
            running = None
            for l in range(a + 1):
                term = rhos[a][l] * image[l]
                running = term if running is None else running + term
            row.append(running)
        margins.append(row)
        full = [[margins[max(a, b)][min(a, b)] for b in range(t + 1)] for a in range(t + 1)]
        mixing = spd_mixing(full)
        following = [zero]
        for k in range(ITERS):
            running = zero
            for a in range(t + 1):
                if k <= a:
                    running = running + mixing[a] * rhos[a][k]
            following.append(running)
        rhos.append(following)
    return rhos[ITERS]


def kernel(
    n_gx,
    n_gy,
    x_hbm,
    solute_hbm,
    exposure_hbm,
    offset_hbm,
    row_hbm,
    live_hbm,
    coupling_hbm,
    cell_hbm,
    evaluation_hbm,
    projection_hbm,
    far_hbm,
    out_ref,
    solute,
    exposure,
    offset,
    row,
    live,
    coupling,
    cell,
    evaluation,
    projection,
    far,
    y,
    z,
    slots,
    whigh,
    wlow,
    source,
    member,
    onehot,
    farhigh,
    farlow,
    kghigh,
    kglow,
    near_cells,
    halo,
    mine,
    part_in,
    plane,
    mid_in,
    whole,
    moments,
    counts,
    scaled,
    expanded,
    unit,
    pair_out,
    pair_in,
    gram_out,
    gram_in,
    load_sem,
    halo_send,
    halo_recv,
    cell_send,
    cell_recv,
    part_send,
    part_recv,
    mid_send,
    mid_recv,
    whole_send,
    whole_recv,
    gram_send,
    gram_recv,
):
    gx = lax.axis_index("gx")
    gy = lax.axis_index("gy")
    piece = LANES // n_gy

    def peer_y(step):
        return (gx, lax.rem(gy + step, n_gy))

    def peer_x(step):
        return (lax.rem(gx + step, n_gx), gy)

    def beside(index):
        dx, dy = AROUND[index]
        return (lax.rem(gx + dx + n_gx, n_gx), lax.rem(gy + dy + n_gy, n_gy))

    def greet(device):
        pl.semaphore_signal(barrier, inc=1, device_id=device, device_id_type=MESH)

    def each(first, last, act):
        def one(step, carry):
            act(step)
            return carry

        lax.fori_loop(first, last, one, 0)

    def every(count, act):
        start = max(0, 3 * count // 8 - 1)
        each(0, count - 1, lambda i: act(lax.rem(i + start, count - 1) + 1))

    barrier = pltpu.get_barrier_semaphore()
    every(n_gx, lambda step: greet(peer_x(step)))
    every(n_gy, lambda step: greet(peer_y(step)))
    corners = [i for i, (dx, dy) in enumerate(AROUND) if dx != 0 and dy != 0]
    for i in corners:
        greet(beside(i))

    loads = [
        pltpu.make_async_copy(there, here, load_sem.at[i])
        for i, (there, here) in enumerate(
            [
                (cell_hbm, cell),
                (offset_hbm, offset),
                (row_hbm, row),
                (live_hbm, live),
                (coupling_hbm, coupling),
                (x_hbm, z.at[0]),
                (x_hbm, y.at[0]),
                (far_hbm, far),
                (evaluation_hbm, evaluation),
                (exposure_hbm, exposure),
                (projection_hbm, projection),
                (solute_hbm, solute),
            ]
        )
    ]
    for load in loads:
        load.start()
    def bytes_of(ref, sem):
        return pltpu.make_async_copy(ref, ref, sem)

    def halo_copy(k, index):
        return pltpu.make_async_remote_copy(
            src_ref=z.at[k, pl.ds(0, EDGE)],
            dst_ref=halo.at[k, pl.ds((7 - index) * EDGE, EDGE)],
            send_sem=halo_send.at[k, index],
            recv_sem=halo_recv.at[k, 7 - index],
            device_id=beside(index),
            device_id_type=MESH,
        )

    def cell_copy(index):
        return pltpu.make_async_remote_copy(
            src_ref=near_cells.at[8],
            dst_ref=near_cells.at[7 - index],
            send_sem=cell_send.at[index],
            recv_sem=cell_recv.at[7 - index],
            device_id=beside(index),
            device_id_type=MESH,
        )

    def part_copy(k, step):
        return pltpu.make_async_remote_copy(
            src_ref=mine.at[k, lax.rem(gy + step, n_gy)],
            dst_ref=part_in.at[k, step],
            send_sem=part_send.at[k],
            recv_sem=part_recv.at[k],
            device_id=peer_y(step),
            device_id_type=MESH,
        )

    def mid_copy(k, step):
        return pltpu.make_async_remote_copy(
            src_ref=plane.at[k],
            dst_ref=mid_in.at[k, step],
            send_sem=mid_send.at[k],
            recv_sem=mid_recv.at[k],
            device_id=peer_x(step),
            device_id_type=MESH,
        )

    def whole_copy(k, step):
        return pltpu.make_async_remote_copy(
            src_ref=whole.at[k, gy],
            dst_ref=whole.at[k, gy],
            send_sem=whole_send.at[k],
            recv_sem=whole_recv.at[k],
            device_id=peer_y(step),
            device_id_type=MESH,
        )

    def gram_copy(step):
        return pltpu.make_async_remote_copy(
            src_ref=gram_out.at[0],
            dst_ref=gram_in.at[step],
            send_sem=gram_send.at[0],
            recv_sem=gram_recv.at[0],
            device_id=(
                lax.rem(gx + step // (n_gy // 2), n_gx),
                lax.rem(gy + 2 * (step % (n_gy // 2)), n_gy),
            ),
            device_id_type=MESH,
        )

    def pair_copy():
        return pltpu.make_async_remote_copy(
            src_ref=pair_out.at[0],
            dst_ref=pair_in.at[0],
            send_sem=gram_send.at[1],
            recv_sem=gram_recv.at[1],
            device_id=(gx, gy + 1 - 2 * lax.rem(gy, 2)),
            device_id_type=MESH,
        )

    def sent(k):
        for i in range(8):
            halo_copy(k, i).wait_send()
        peers = pl.ds(0, n_gy - 1)
        bytes_of(mine.at[k, peers], part_send.at[k]).wait()
        bytes_of(mid_in.at[k, pl.ds(1, n_gx - 1)], mid_send.at[k]).wait()
        bytes_of(whole.at[k, peers], whole_send.at[k]).wait()

    def prepare(k):
        first = z[k].T[:Q]
        high, rest = split(first)
        middle, last = split(first - high.astype(F32))
        ones = jnp.ones((Q, SPH), BF16)
        stacked = jnp.concatenate([high, middle, last, ones], axis=0)
        parts = dot(stacked, member[...], NT)
        number = parts[3 * Q : 3 * Q + 1]
        parts = parts[:Q] + parts[Q : 2 * Q] + parts[2 * Q : 3 * Q]
        for t in range(TILES):
            columns = slice(t * LANES, (t + 1) * LANES)
            if piece >= Q:
                fold = piece // Q
                mine[k, t // fold, (t % fold) * Q : (t % fold + 1) * Q, :] = parts[:, columns]
                at = piece + t % fold
                mine[k, t // fold, at : at + 1, :] = number[:, columns]
            else:
                per = Q // piece
                for j in range(per):
                    mine[k, t * per + j, :piece, :] = parts[j * piece : (j + 1) * piece, columns]
                    mine[k, t * per + j, piece : piece + 1, :] = number[:, columns]

    def send_halo(k):
        for index in FARTHEST:
            halo_copy(k, index).start()

    def send_part(k):
        every(n_gy, lambda step: part_copy(k, step).start())

    def pass_on(k):
        bytes_of(part_in.at[k, pl.ds(1, n_gy - 1)], part_recv.at[k]).wait()
        plane[k] = jnp.sum(part_in[k, 1:], axis=0) + mine[k, gy]
        every(n_gx, lambda step: mid_copy(k, step).start())

    def spread(k):
        bytes_of(mid_in.at[k, pl.ds(1, n_gx - 1)], mid_recv.at[k]).wait()
        whole[k, gy] = jnp.sum(mid_in[k, 1:], axis=0) + plane[k]
        every(n_gy, lambda step: whole_copy(k, step).start())

    index = lax.broadcasted_iota(jnp.int32, (1, H), 1)
    degree = jnp.zeros((1, H), F32)
    for n in range(1, LMAX + 1):
        degree = degree + (index >= n * n).astype(F32)
    scale = jnp.where(index < (LMAX + 1) ** 2, (2.0 * degree + 1.0) / (4.0 * math.pi), 0.0)
    component = lax.broadcasted_iota(jnp.int32, (Q, NC), 0)
    moment_degree = jnp.zeros((Q, NC), F32)
    for n in range(1, 4):
        moment_degree = moment_degree + (component >= n * n).astype(F32)
    moment_scale = (2.0 * moment_degree + 1.0) / (4.0 * math.pi)

    def gathered(k):
        bytes_of(whole.at[k, pl.ds(0, n_gy - 1)], whole_recv.at[k]).wait()
        for t in range(TILES):
            columns = slice(t * LANES, (t + 1) * LANES)
            if piece >= Q:
                fold = piece // Q
                moments[:, columns] = whole[k, t // fold, (t % fold) * Q : (t % fold + 1) * Q, :]
                at = piece + t % fold
                counts[:, columns] = whole[k, t // fold, at : at + 1, :]
            else:
                per = Q // piece
                for j in range(per):
                    moments[j * piece : (j + 1) * piece, columns] = whole[k, t * per + j, :piece, :]
                counts[:, columns] = whole[k, t * per, piece : piece + 1, :]
        value = moment_scale * (moments[...] - counts[...] * expanded[...])
        scaled[...] = value
        return jnp.concatenate(split(value), axis=0)

    def distant(both, count):
        sums = dot(both, kghigh[:, :count])
        sums = sums[:Q] + sums[Q:] + dot(both[:Q], kglow[:, :count])
        blank = jnp.zeros((LANES - Q, LANES), F32)
        blocks = [
            jnp.concatenate([sums[:, at : at + LANES], blank], axis=0).T
            for at in range(0, count, LANES)
        ]
        return jnp.concatenate(blocks, axis=0)

    def expand():
        high, low = split(scaled[...])
        both = dot(jnp.concatenate([high, low], axis=0), farhigh[...])
        expanded[...] = both[:Q] + both[Q:] + dot(high, farlow[...])

    def far_columns(at, chosen):
        columns = slice(at, at + SPH)

        def one(step):
            block = pl.ds(pl.multiple_of(step * SPH, SPH), SPH)
            kghigh[block, columns] = dot(farhigh[block, :], chosen[...]).astype(BF16)
            kglow[block, columns] = dot(farlow[block, :], chosen[...]).astype(BF16)

        each(0, NC // SPH, one)

    def belong(chosen, cells):
        cells = jnp.broadcast_to(cells, (LANES, SPH))
        for t in range(TILES):
            numbers = lax.broadcasted_iota(jnp.int32, (LANES, SPH), 0) + t * LANES
            rows = slice(t * LANES, (t + 1) * LANES)
            chosen[rows, :] = (cells == numbers.astype(F32)).astype(F32).astype(BF16)

    loads[0].wait()
    own_cells = cell[...].astype(F32)
    belong(member, own_cells)
    near_cells[8] = jnp.concatenate([own_cells[:, :EDGE], own_cells[:, :EDGE]], axis=1)

    for i in range(1, 5):
        loads[i].wait()
    offsets = offset[...]
    place = jnp.where(
        offsets == 4,
        row[...],
        SPH + jnp.where(offsets > 4, offsets - 1, offsets) * EDGE + row[...],
    )
    alive = jnp.concatenate(
        [jnp.broadcast_to(live[d : d + 1, :], (SLOTS, SPH)) for d in range(ND)], axis=0
    )
    slot = lax.broadcasted_iota(jnp.int32, (NB, SPH), 0) & (SLOTS - 1)
    weights = jnp.where(slot < alive, coupling[...], 0.0)
    blank = jnp.zeros((LANES - 2 * NB, SPH), F32)
    slots[...] = jnp.concatenate([place.astype(F32), weights, blank], axis=0).T

    block_rows = 16

    def weigh(step):
        base = pl.multiple_of(step * block_rows, block_rows)
        held = slots[pl.ds(base, block_rows), :]
        lanes = lax.broadcasted_iota(jnp.int32, (block_rows, LANES), 1).astype(F32)
        for d in range(ND):
            sums = [jnp.zeros((block_rows, LANES), F32) for t in range(SRC // LANES)]
            for s in range(d * SLOTS, (d + 1) * SLOTS):
                where = jnp.broadcast_to(held[:, s : s + 1], (block_rows, LANES))
                value = jnp.broadcast_to(held[:, NB + s : NB + s + 1], (block_rows, LANES))
                for t in range(SRC // LANES):
                    sums[t] = sums[t] + jnp.where(where == lanes + t * LANES, value, 0.0)
            high, low = split(jnp.concatenate(sums, axis=1))
            rows = pl.ds(pl.multiple_of(d * SPH + base, block_rows), block_rows)
            whigh[rows, :] = high
            wlow[rows, :] = low


    loads[5].wait()
    prepare(0)
    pl.semaphore_wait(barrier, (n_gy - 1) + (n_gx - 1) + len(corners))
    send_part(0)
    send_halo(0)
    for i in range(8):
        cell_copy(i).start()
    each(0, SPH // block_rows, weigh)

    loads[7].wait()
    for t in range(TILES):
        rows = slice(t * LANES, (t + 1) * LANES)
        high, low = split(far[rows, :])
        farhigh[rows, :] = high
        farlow[rows, :] = low
    expanded[...] = jnp.zeros_like(expanded)
    for load in loads[8:] + loads[6:7]:
        load.wait()
    evaluation_parts = jnp.concatenate(split(evaluation[...]), axis=1)
    projection_parts = jnp.concatenate(split(projection[...]), axis=1)
    lane = lax.broadcasted_iota(jnp.int32, (1, LANES), 1)

    def product(left, right):
        high, low = split(left)
        both = dot(high, right)
        return both[:, :H] + both[:, H:] + dot(low, right[:, :H])

    def neighbour_cells(first):
        pairs = [
            jnp.where(lane < EDGE, near_cells[at], near_cells[at + 1])
            for at in (first, first + 2)
        ]
        return jnp.concatenate(pairs, axis=1)

    def put(rows, value):
        high, low = split(value)
        source[rows, :H] = high
        source[rows, H:] = low

    def iterate(k, carry):
        @pl.when(k == 1)
        def _():
            for i in range(8):
                cell_copy(i).wait_recv()
            belong(onehot, neighbour_cells(0))
            far_columns(SPH, onehot)

        @pl.when(k > 0)
        def _():
            spread(k - 1)

        @pl.when(k > 1)
        def _():
            expand()

        @pl.when(k == 1)
        def _():
            belong(onehot, neighbour_cells(4))
            far_columns(2 * SPH, onehot)

        pass_on(k)

        @pl.when(k == 1)
        def _():
            far_columns(0, member)

        for i in range(8):
            halo_copy(k, i).wait_recv()

        @pl.when(k == 0)
        def _():
            put(slice(0, SPH), y[0])
            put(slice(SPH, SRC), halo[0])

        @pl.when(k > 0)
        def _():
            taken = distant(gathered(k - 1), SRC)
            own = z[k] - taken[:SPH]
            y[k] = own
            put(slice(0, SPH), own)
            put(slice(SPH, SRC), halo[k] - taken[SPH:])

        potential = jnp.zeros((SPH, H), F32)
        for pair in range(ND // 2):
            sums = []
            for d in (2 * pair, 2 * pair + 1):
                rows = slice(d * SPH, (d + 1) * SPH)
                both = dot(whigh[rows, :], source[...])
                low = dot(wlow[rows, :], source[:, :H])
                sums.append(both[:, :H] + both[:, H:] + low)
            rows = slice(2 * pair * H, 2 * (pair + 1) * H)
            potential = potential + product(
                jnp.concatenate(sums, axis=1), evaluation_parts[rows]
            )
        nearby = product(potential * exposure[...], projection_parts)
        z[k + 1] = scale * (solute[...] - nearby)

        @pl.when(k < ITERS - 1)
        def _():
            @pl.when(k == 1)
            def _():
                send_halo(k + 1)

            prepare(k + 1)
            send_part(k + 1)

            @pl.when(k != 1)
            def _():
                send_halo(k + 1)

        return carry

    lax.fori_loop(0, ITERS, iterate, 0)

    spread(ITERS - 1)
    expand()
    pairs = [(a, b) for a in range(ITERS) for b in range(a + 1)]
    early = [y[k + 1] - y[k] for k in range(ITERS - 1)]
    height = jnp.abs(early[0])
    for change in early[1:]:
        height = jnp.maximum(height, jnp.abs(change))
    top = largest(height)
    top = jnp.where(top > 0.0, top, 1.0)
    inverse = 1.0 / top
    for k in range(ITERS - 1):
        unit[k] = early[k] * inverse
    line = jnp.zeros((1, LANES), F32)
    for i, (a, b) in enumerate(pairs):
        if a < ITERS - 1:
            line = line + jnp.where(lane == i, total(unit[a] * unit[b]), 0.0)

    last = z[ITERS] - distant(gathered(ITERS - 1), SPH)
    y[ITERS] = last
    change = last - y[ITERS - 1]
    most = jnp.maximum(top, largest(jnp.abs(change)))
    ratio = top / most
    change = change * (1.0 / most)
    line = line * (ratio * ratio)
    for i, (a, b) in enumerate(pairs):
        if a == ITERS - 1:
            sums = total(change * change) if b == a else total(change * unit[b]) * ratio
            line = line + jnp.where(lane == i, sums, 0.0)
    line = jnp.where(lane == len(pairs), most, line)
    def merged(lines):
        tops = lines[:, len(pairs) : len(pairs) + 1]
        most = jnp.max(tops, axis=0, keepdims=True)
        ratio = tops / most
        sums = jnp.sum(lines * (ratio * ratio), axis=0, keepdims=True)
        return jnp.where(lane == len(pairs), most, sums)

    pair_out[0] = line
    pair_copy().start()
    pair_copy().wait_recv()
    line = merged(jnp.concatenate([line, pair_in[0]], axis=0))
    gram_out[0] = line
    gram_in[0] = line
    chips = n_gx * n_gy // 2
    columns = n_gy // 2
    for row in sorted(range(n_gx), key=lambda row: -min(row, n_gx - row)):
        first = row * columns
        each(max(first, 1), first + columns, lambda step: gram_copy(step).start())
    each(0, ITERS, sent)
    for i in range(8):
        cell_copy(i).wait_send()
    pair_copy().wait_send()
    bytes_of(gram_in.at[pl.ds(1, chips - 1)], gram_recv.at[0]).wait()
    line = merged(gram_in[...].reshape(chips, LANES))

    gram = [[None] * ITERS for a in range(ITERS)]
    for i, (a, b) in enumerate(pairs):
        gram[a][b] = line[:, i : i + 1]
    rho = mixed_coefficients(gram)
    mixed = rho[1] * y[1]
    for k in range(2, ITERS + 1):
        mixed = mixed + rho[k] * y[k]
    out_ref[...] = mixed

    bytes_of(gram_in.at[pl.ds(1, chips - 1)], gram_send.at[0]).wait()


def per_device(
    n_gx,
    n_gy,
    start_charges,
    solute_field,
    exposure,
    owner_offset,
    owner_row,
    live_slots,
    coupling,
    cell_index,
    evaluation,
    projection,
    far_kernel,
):
    hbm = pl.BlockSpec(memory_space=pl.ANY)
    piece = LANES // n_gy
    rows = piece + max(1, piece // Q)
    dma = pltpu.SemaphoreType.DMA

    def held(*shape, dtype=F32):
        return pltpu.VMEM(shape, dtype)

    return pl.pallas_call(
        functools.partial(kernel, n_gx, n_gy),
        out_shape=jax.ShapeDtypeStruct((SPH, H), F32),
        in_specs=[hbm] * 11,
        out_specs=pl.BlockSpec(memory_space=pltpu.VMEM),
        scratch_shapes=[
            held(SPH, H),
            held(SPH, H),
            held(NB, SPH, dtype=jnp.int32),
            held(NB, SPH, dtype=jnp.int32),
            held(ND, SPH, dtype=jnp.int32),
            held(NB, SPH),
            held(1, SPH, dtype=jnp.int32),
            held(ND * H, H),
            held(H, H),
            held(NC, NC),
            held(ITERS + 1, SPH, H),
            held(ITERS + 1, SPH, H),
            held(SPH, LANES),
            held(ND * SPH, SRC, dtype=BF16),
            held(ND * SPH, SRC, dtype=BF16),
            held(SRC, 2 * H, dtype=BF16),
            held(NC, SPH, dtype=BF16),
            held(NC, SPH, dtype=BF16),
            held(NC, NC, dtype=BF16),
            held(NC, NC, dtype=BF16),
            held(NC, SRC, dtype=BF16),
            held(NC, SRC, dtype=BF16),
            held(9, 1, LANES),
            held(ITERS, 8 * EDGE, H),
            held(ITERS, n_gy, rows, LANES),
            held(ITERS, n_gy, rows, LANES),
            held(ITERS, rows, LANES),
            held(ITERS, n_gx, rows, LANES),
            held(ITERS, n_gy, rows, LANES),
            held(Q, NC),
            held(1, NC),
            held(Q, NC),
            held(Q, NC),
            held(ITERS - 1, SPH, H),
            held(1, 1, LANES),
            held(1, 1, LANES),
            held(1, 1, LANES),
            held(n_gx * n_gy // 2, 1, LANES),
            dma((12,)),
            dma((ITERS, 8)),
            dma((ITERS, 8)),
            dma((8,)),
            dma((8,)),
            dma((ITERS,)),
            dma((ITERS,)),
            dma((ITERS,)),
            dma((ITERS,)),
            dma((ITERS,)),
            dma((ITERS,)),
            dma((2,)),
            dma((2,)),
        ],
        compiler_params=pltpu.CompilerParams(
            collective_id=0, has_side_effects=True, vmem_limit_bytes=48 * 1024 * 1024
        ),
        name="screening",
    )(
        *[
            pltpu.with_memory_space_constraint(a, pltpu.HBM)
            for a in (
        start_charges,
        solute_field,
        exposure,
        owner_offset.T,
        owner_row.T,
        live_slots.T,
        coupling.T,
        cell_index.reshape(1, SPH),
        evaluation,
        projection,
        far_kernel,
            )
        ]
    )


def solution(mesh):
    placed = (
        P(("gx", "gy"), None),
        P(("gx", "gy"), None),
        P(("gx", "gy"), None),
        P(("gx", "gy"), None),
        P(("gx", "gy"), None),
        P(("gx", "gy"), None),
        P(("gx", "gy"), None),
        P(("gx", "gy")),
        P(),
        P(),
        P(),
    )
    return jax.shard_map(
        functools.partial(per_device, mesh.shape["gx"], mesh.shape["gy"]),
        mesh=mesh,
        in_specs=placed,
        out_specs=P(("gx", "gy"), None),
        check_vma=False,
    )
```

```python
import functools
import math

import jax
import jax.numpy as jnp
from jax import lax
from jax.experimental import pallas as pl
from jax.experimental.pallas import tpu as pltpu
from jax.sharding import PartitionSpec as P

MESH = pl.DeviceIdType.MESH
F32 = jnp.float32
BF16 = jnp.bfloat16

LMAX = 10
H = 128
Q = 16
ND = 4
SLOTS = 8
NB = 32
EDGE = 64
ITERS = 4
SPH = 256
NC = 1024
SRC = SPH + 8 * EDGE
LANES = 128
TILES = NC // LANES
AROUND = [(dx, dy) for dx in (-1, 0, 1) for dy in (-1, 0, 1) if (dx, dy) != (0, 0)]
FARTHEST = (0, 2, 5, 7, 1, 6, 3, 4)
NN = (((1,), (0,)), ((), ()))
NT = (((1,), (1,)), ((), ()))


def spd_mixing(margins):
    order = len(margins)
    diagonal_sum = margins[0][0]
    for a in range(1, order):
        diagonal_sum = diagonal_sum + margins[a][a]
    damping = 0.01 * diagonal_sum / order
    triangle = [[None] * order for a in range(order)]
    for a in range(order):
        for b in range(a + 1):
            running = margins[a][b] + (damping if a == b else 0.0)
            for c in range(b):
                running = running - triangle[a][c] * triangle[b][c]
            if a == b:
                triangle[a][a] = jnp.sqrt(running)
            else:
                triangle[a][b] = running / triangle[b][b]
    forward = []
    for a in range(order):
        running = jnp.ones_like(diagonal_sum)
        for c in range(a):
            running = running - triangle[a][c] * forward[c]
        forward.append(running / triangle[a][a])
    backward = [None] * order
    for a in reversed(range(order)):
        running = forward[a]
        for c in range(a + 1, order):
            running = running - triangle[c][a] * backward[c]
        backward[a] = running / triangle[a][a]
    weight_sum = backward[0]
    for a in range(1, order):
        weight_sum = weight_sum + backward[a]
    return [value / weight_sum for value in backward]


def split(value):
    high = value.astype(BF16)
    return high, (value - high.astype(F32)).astype(BF16)


def dot(a, b, dims=NN):
    return lax.dot_general(a, b, dims, preferred_element_type=F32)


def total(value):
    rows = jnp.sum(value.reshape(-1, 8, LANES), axis=0)
    return jnp.sum(jnp.sum(rows, axis=0, keepdims=True), axis=1, keepdims=True)


def largest(value):
    rows = jnp.max(value.reshape(-1, 8, LANES), axis=0)
    return jnp.max(jnp.max(rows, axis=0, keepdims=True), axis=1, keepdims=True)


def mixed_coefficients(gram):
    zero = jnp.zeros_like(gram[0][0])
    one = jnp.ones_like(zero)
    rhos = [[one] + [zero] * ITERS]
    margins = []
    for t in range(ITERS):
        new = rhos[t]
        image = []
        for l in range(ITERS):
            running = None
            for k in range(t + 1):
                term = new[k] * gram[max(k, l)][min(k, l)]
                running = term if running is None else running + term
            image.append(running)
        row = []
        for a in range(t + 1):
            running = None
            for l in range(a + 1):
                term = rhos[a][l] * image[l]
                running = term if running is None else running + term
            row.append(running)
        margins.append(row)
        full = [[margins[max(a, b)][min(a, b)] for b in range(t + 1)] for a in range(t + 1)]
        mixing = spd_mixing(full)
        following = [zero]
        for k in range(ITERS):
            running = zero
            for a in range(t + 1):
                if k <= a:
                    running = running + mixing[a] * rhos[a][k]
            following.append(running)
        rhos.append(following)
    return rhos[ITERS]


def kernel(
    n_gx,
    n_gy,
    x_hbm,
    solute_hbm,
    exposure_hbm,
    offset_hbm,
    row_hbm,
    live_hbm,
    coupling_hbm,
    cell_hbm,
    evaluation_hbm,
    projection_hbm,
    far_hbm,
    out_ref,
    solute,
    exposure,
    offset,
    row,
    live,
    coupling,
    cell,
    evaluation,
    projection,
    far,
    y,
    z,
    slots,
    whigh,
    wlow,
    source,
    member,
    onehot,
    farhigh,
    farlow,
    kghigh,
    kglow,
    near_cells,
    halo,
    mine,
    part_in,
    plane,
    mid_in,
    whole,
    moments,
    counts,
    scaled,
    expanded,
    unit,
    pair_out,
    pair_in,
    gram_out,
    gram_in,
    load_sem,
    halo_send,
    halo_recv,
    cell_send,
    cell_recv,
    part_send,
    part_recv,
    mid_send,
    mid_recv,
    whole_send,
    whole_recv,
    gram_send,
    gram_recv,
):
    gx = lax.axis_index("gx")
    gy = lax.axis_index("gy")
    piece = LANES // n_gy

    def peer_y(step):
        return (gx, lax.rem(gy + step, n_gy))

    def peer_x(step):
        return (lax.rem(gx + step, n_gx), gy)

    def beside(index):
        dx, dy = AROUND[index]
        return (lax.rem(gx + dx + n_gx, n_gx), lax.rem(gy + dy + n_gy, n_gy))

    def greet(device):
        pl.semaphore_signal(barrier, inc=1, device_id=device, device_id_type=MESH)

    def each(first, last, act):
        def one(step, carry):
            act(step)
            return carry

        lax.fori_loop(first, last, one, 0)

    def every(count, act):
        start = max(0, 3 * count // 8 - 1)
        each(0, count - 1, lambda i: act(lax.rem(i + start, count - 1) + 1))

    barrier = pltpu.get_barrier_semaphore()
    every(n_gx, lambda step: greet(peer_x(step)))
    every(n_gy, lambda step: greet(peer_y(step)))
    corners = [i for i, (dx, dy) in enumerate(AROUND) if dx != 0 and dy != 0]
    for i in corners:
        greet(beside(i))

    loads = [
        pltpu.make_async_copy(there, here, load_sem.at[i])
        for i, (there, here) in enumerate(
            [
                (cell_hbm, cell),
                (offset_hbm, offset),
                (row_hbm, row),
                (live_hbm, live),
                (coupling_hbm, coupling),
                (x_hbm, z.at[0]),
                (x_hbm, y.at[0]),
                (far_hbm, far),
                (evaluation_hbm, evaluation),
                (exposure_hbm, exposure),
                (projection_hbm, projection),
                (solute_hbm, solute),
            ]
        )
    ]
    for load in loads:
        load.start()
    def bytes_of(ref, sem):
        return pltpu.make_async_copy(ref, ref, sem)

    def halo_copy(k, index):
        return pltpu.make_async_remote_copy(
            src_ref=z.at[k, pl.ds(0, EDGE)],
            dst_ref=halo.at[k, pl.ds((7 - index) * EDGE, EDGE)],
            send_sem=halo_send.at[k, index],
            recv_sem=halo_recv.at[k, 7 - index],
            device_id=beside(index),
            device_id_type=MESH,
        )

    def cell_copy(index):
        return pltpu.make_async_remote_copy(
            src_ref=near_cells.at[8],
            dst_ref=near_cells.at[7 - index],
            send_sem=cell_send.at[index],
            recv_sem=cell_recv.at[7 - index],
            device_id=beside(index),
            device_id_type=MESH,
        )

    def part_copy(k, step):
        return pltpu.make_async_remote_copy(
            src_ref=mine.at[k, lax.rem(gy + step, n_gy)],
            dst_ref=part_in.at[k, step],
            send_sem=part_send.at[k],
            recv_sem=part_recv.at[k],
            device_id=peer_y(step),
            device_id_type=MESH,
        )

    def mid_copy(k, step):
        return pltpu.make_async_remote_copy(
            src_ref=plane.at[k],
            dst_ref=mid_in.at[k, step],
            send_sem=mid_send.at[k],
            recv_sem=mid_recv.at[k],
            device_id=peer_x(step),
            device_id_type=MESH,
        )

    def whole_copy(k, step):
        return pltpu.make_async_remote_copy(
            src_ref=whole.at[k, gy],
            dst_ref=whole.at[k, gy],
            send_sem=whole_send.at[k],
            recv_sem=whole_recv.at[k],
            device_id=peer_y(step),
            device_id_type=MESH,
        )

    def gram_copy(step):
        return pltpu.make_async_remote_copy(
            src_ref=gram_out.at[0],
            dst_ref=gram_in.at[step],
            send_sem=gram_send.at[0],
            recv_sem=gram_recv.at[0],
            device_id=(
                lax.rem(gx + step // (n_gy // 2), n_gx),
                lax.rem(gy + 2 * (step % (n_gy // 2)), n_gy),
            ),
            device_id_type=MESH,
        )

    def pair_copy():
        return pltpu.make_async_remote_copy(
            src_ref=pair_out.at[0],
            dst_ref=pair_in.at[0],
            send_sem=gram_send.at[1],
            recv_sem=gram_recv.at[1],
            device_id=(gx, gy + 1 - 2 * lax.rem(gy, 2)),
            device_id_type=MESH,
        )

    def sent(k):
        for i in range(8):
            halo_copy(k, i).wait_send()
        peers = pl.ds(0, n_gy - 1)
        bytes_of(mine.at[k, peers], part_send.at[k]).wait()
        bytes_of(mid_in.at[k, pl.ds(1, n_gx - 1)], mid_send.at[k]).wait()
        bytes_of(whole.at[k, peers], whole_send.at[k]).wait()

    def prepare(k):
        first = z[k].T[:Q]
        high, rest = split(first)
        middle, last = split(first - high.astype(F32))
        ones = jnp.ones((Q, SPH), BF16)
        stacked = jnp.concatenate([high, middle, last, ones], axis=0)
        parts = dot(stacked, member[...], NT)
        number = parts[3 * Q : 3 * Q + 1]
        parts = parts[:Q] + parts[Q : 2 * Q] + parts[2 * Q : 3 * Q]
        for t in range(TILES):
            columns = slice(t * LANES, (t + 1) * LANES)
            if piece >= Q:
                fold = piece // Q
                mine[k, t // fold, (t % fold) * Q : (t % fold + 1) * Q, :] = parts[:, columns]
                at = piece + t % fold
                mine[k, t // fold, at : at + 1, :] = number[:, columns]
            else:
                per = Q // piece
                for j in range(per):
                    mine[k, t * per + j, :piece, :] = parts[j * piece : (j + 1) * piece, columns]
                    mine[k, t * per + j, piece : piece + 1, :] = number[:, columns]

    def send_halo(k):
        for index in FARTHEST:
            halo_copy(k, index).start()

    def send_part(k):
        every(n_gy, lambda step: part_copy(k, step).start())

    def pass_on(k):
        bytes_of(part_in.at[k, pl.ds(1, n_gy - 1)], part_recv.at[k]).wait()
        plane[k] = jnp.sum(part_in[k, 1:], axis=0) + mine[k, gy]
        every(n_gx, lambda step: mid_copy(k, step).start())

    def spread(k):
        bytes_of(mid_in.at[k, pl.ds(1, n_gx - 1)], mid_recv.at[k]).wait()
        whole[k, gy] = jnp.sum(mid_in[k, 1:], axis=0) + plane[k]
        every(n_gy, lambda step: whole_copy(k, step).start())

    index = lax.broadcasted_iota(jnp.int32, (1, H), 1)
    degree = jnp.zeros((1, H), F32)
    for n in range(1, LMAX + 1):
        degree = degree + (index >= n * n).astype(F32)
    scale = jnp.where(index < (LMAX + 1) ** 2, (2.0 * degree + 1.0) / (4.0 * math.pi), 0.0)
    component = lax.broadcasted_iota(jnp.int32, (Q, NC), 0)
    moment_degree = jnp.zeros((Q, NC), F32)
    for n in range(1, 4):
        moment_degree = moment_degree + (component >= n * n).astype(F32)
    moment_scale = (2.0 * moment_degree + 1.0) / (4.0 * math.pi)

    def gathered(k):
        bytes_of(whole.at[k, pl.ds(0, n_gy - 1)], whole_recv.at[k]).wait()
        for t in range(TILES):
            columns = slice(t * LANES, (t + 1) * LANES)
            if piece >= Q:
                fold = piece // Q
                moments[:, columns] = whole[k, t // fold, (t % fold) * Q : (t % fold + 1) * Q, :]
                at = piece + t % fold
                counts[:, columns] = whole[k, t // fold, at : at + 1, :]
            else:
                per = Q // piece
                for j in range(per):
                    moments[j * piece : (j + 1) * piece, columns] = whole[k, t * per + j, :piece, :]
                counts[:, columns] = whole[k, t * per, piece : piece + 1, :]
        value = moment_scale * (moments[...] - counts[...] * expanded[...])
        scaled[...] = value
        return jnp.concatenate(split(value), axis=0)

    def distant(both, count):
        sums = dot(both, kghigh[:, :count])
        sums = sums[:Q] + sums[Q:] + dot(both[:Q], kglow[:, :count])
        blank = jnp.zeros((LANES - Q, LANES), F32)
        blocks = [
            jnp.concatenate([sums[:, at : at + LANES], blank], axis=0).T
            for at in range(0, count, LANES)
        ]
        return jnp.concatenate(blocks, axis=0)

    def expand():
        high, low = split(scaled[...])
        both = dot(jnp.concatenate([high, low], axis=0), farhigh[...])
        expanded[...] = both[:Q] + both[Q:] + dot(high, farlow[...])

    def far_columns(at, chosen):
        columns = slice(at, at + SPH)

        def one(step):
            block = pl.ds(pl.multiple_of(step * SPH, SPH), SPH)
            kghigh[block, columns] = dot(farhigh[block, :], chosen[...]).astype(BF16)
            kglow[block, columns] = dot(farlow[block, :], chosen[...]).astype(BF16)

        each(0, NC // SPH, one)

    def belong(chosen, cells):
        cells = jnp.broadcast_to(cells, (LANES, SPH))
        for t in range(TILES):
            numbers = lax.broadcasted_iota(jnp.int32, (LANES, SPH), 0) + t * LANES
            rows = slice(t * LANES, (t + 1) * LANES)
            chosen[rows, :] = (cells == numbers.astype(F32)).astype(F32).astype(BF16)

    loads[0].wait()
    own_cells = cell[...].astype(F32)
    belong(member, own_cells)
    near_cells[8] = jnp.concatenate([own_cells[:, :EDGE], own_cells[:, :EDGE]], axis=1)

    for i in range(1, 5):
        loads[i].wait()
    offsets = offset[...]
    place = jnp.where(
        offsets == 4,
        row[...],
        SPH + jnp.where(offsets > 4, offsets - 1, offsets) * EDGE + row[...],
    )
    alive = jnp.concatenate(
        [jnp.broadcast_to(live[d : d + 1, :], (SLOTS, SPH)) for d in range(ND)], axis=0
    )
    slot = lax.broadcasted_iota(jnp.int32, (NB, SPH), 0) & (SLOTS - 1)
    weights = jnp.where(slot < alive, coupling[...], 0.0)
    blank = jnp.zeros((LANES - 2 * NB, SPH), F32)
    slots[...] = jnp.concatenate([place.astype(F32), weights, blank], axis=0).T

    block_rows = 16

    def weigh(first, count, step):
        base = pl.multiple_of(step * block_rows, block_rows)
        held = slots[pl.ds(base, block_rows), :]
        lanes = lax.broadcasted_iota(jnp.int32, (block_rows, LANES), 1).astype(F32)
        for d in range(ND):
            sums = [jnp.zeros((block_rows, LANES), F32) for t in range(SRC // LANES)]
            for s in range(d * SLOTS, (d + 1) * SLOTS):
                where = jnp.broadcast_to(held[:, s : s + 1], (block_rows, LANES))
                value = jnp.broadcast_to(held[:, NB + s : NB + s + 1], (block_rows, LANES))
                for t in range(SRC // LANES):
                    sums[t] = sums[t] + jnp.where(where == lanes + t * LANES, value, 0.0)
            high, low = split(jnp.concatenate(sums, axis=1))
            at = ND * first + d * count + base - first
            rows = pl.ds(pl.multiple_of(at, block_rows), block_rows)
            whigh[rows, :] = high
            wlow[rows, :] = low


    loads[5].wait()
    prepare(0)
    pl.semaphore_wait(barrier, (n_gy - 1) + (n_gx - 1) + len(corners))
    send_part(0)
    send_halo(0)
    for i in range(8):
        cell_copy(i).start()
    each(0, EDGE // block_rows, functools.partial(weigh, 0, EDGE))
    each(EDGE // block_rows, SPH // block_rows, functools.partial(weigh, EDGE, SPH - EDGE))

    loads[7].wait()
    for t in range(TILES):
        rows = slice(t * LANES, (t + 1) * LANES)
        high, low = split(far[rows, :])
        farhigh[rows, :] = high
        farlow[rows, :] = low
    expanded[...] = jnp.zeros_like(expanded)
    for load in loads[8:] + loads[6:7]:
        load.wait()
    evaluation_parts = jnp.concatenate(split(evaluation[...]), axis=1)
    projection_parts = jnp.concatenate(split(projection[...]), axis=1)
    lane = lax.broadcasted_iota(jnp.int32, (1, LANES), 1)

    def product(left, right):
        high, low = split(left)
        both = dot(high, right)
        return both[:, :H] + both[:, H:] + dot(low, right[:, :H])

    def neighbour_cells(first):
        pairs = [
            jnp.where(lane < EDGE, near_cells[at], near_cells[at + 1])
            for at in (first, first + 2)
        ]
        return jnp.concatenate(pairs, axis=1)

    def put(rows, value):
        high, low = split(value)
        source[rows, :H] = high
        source[rows, H:] = low

    def update(k, *ranges):
        begin, end = ranges[0][0], sum(ranges[-1])
        rows = slice(ND * begin, ND * end)
        both = dot(whigh[rows, :], source[...])
        sums = both[:, :H] + both[:, H:] + dot(wlow[rows, :], source[:, :H])
        blocks = []
        for first, count in ranges:
            at = ND * (first - begin)
            parts = [sums[at + d * count : at + (d + 1) * count] for d in range(ND)]
            blocks.append(jnp.concatenate(parts, axis=1))
        chosen = slice(begin, end)
        potential = product(jnp.concatenate(blocks, axis=0), evaluation_parts)
        nearby = product(potential * exposure[chosen, :], projection_parts)
        z[k + 1, chosen, :] = scale * (solute[chosen, :] - nearby)

    def iterate(k, carry):
        @pl.when(k == 1)
        def _():
            for i in range(8):
                cell_copy(i).wait_recv()
            belong(onehot, neighbour_cells(0))
            far_columns(SPH, onehot)

        @pl.when(k > 0)
        def _():
            spread(k - 1)

        @pl.when(k > 1)
        def _():
            expand()

        @pl.when(k == 1)
        def _():
            belong(onehot, neighbour_cells(4))
            far_columns(2 * SPH, onehot)

        pass_on(k)

        @pl.when(k == 1)
        def _():
            far_columns(0, member)

        for i in range(8):
            halo_copy(k, i).wait_recv()

        @pl.when(k == 0)
        def _():
            put(slice(0, SPH), y[0])
            put(slice(SPH, SRC), halo[0])

        @pl.when(k > 0)
        def _():
            taken = distant(gathered(k - 1), SRC)
            own = z[k] - taken[:SPH]
            y[k] = own
            put(slice(0, SPH), own)
            put(slice(SPH, SRC), halo[k] - taken[SPH:])

        edge, others = (0, EDGE), (EDGE, SPH - EDGE)

        @pl.when(k == 1)
        def _():
            update(k, edge)
            send_halo(k + 1)
            update(k, others)

        @pl.when(k != 1)
        def _():
            update(k, edge, others)

        @pl.when(k < ITERS - 1)
        def _():
            prepare(k + 1)
            send_part(k + 1)

            @pl.when(k != 1)
            def _():
                send_halo(k + 1)

        return carry

    lax.fori_loop(0, ITERS, iterate, 0)

    spread(ITERS - 1)
    expand()
    pairs = [(a, b) for a in range(ITERS) for b in range(a + 1)]
    early = [y[k + 1] - y[k] for k in range(ITERS - 1)]
    height = jnp.abs(early[0])
    for change in early[1:]:
        height = jnp.maximum(height, jnp.abs(change))
    top = largest(height)
    top = jnp.where(top > 0.0, top, 1.0)
    inverse = 1.0 / top
    for k in range(ITERS - 1):
        unit[k] = early[k] * inverse
    line = jnp.zeros((1, LANES), F32)
    for i, (a, b) in enumerate(pairs):
        if a < ITERS - 1:
            line = line + jnp.where(lane == i, total(unit[a] * unit[b]), 0.0)

    last = z[ITERS] - distant(gathered(ITERS - 1), SPH)
    y[ITERS] = last
    change = last - y[ITERS - 1]
    most = jnp.maximum(top, largest(jnp.abs(change)))
    ratio = top / most
    change = change * (1.0 / most)
    line = line * (ratio * ratio)
    for i, (a, b) in enumerate(pairs):
        if a == ITERS - 1:
            sums = total(change * change) if b == a else total(change * unit[b]) * ratio
            line = line + jnp.where(lane == i, sums, 0.0)
    line = jnp.where(lane == len(pairs), most, line)
    def merged(lines):
        tops = lines[:, len(pairs) : len(pairs) + 1]
        most = jnp.max(tops, axis=0, keepdims=True)
        ratio = tops / most
        sums = jnp.sum(lines * (ratio * ratio), axis=0, keepdims=True)
        return jnp.where(lane == len(pairs), most, sums)

    pair_out[0] = line
    pair_copy().start()
    pair_copy().wait_recv()
    line = merged(jnp.concatenate([line, pair_in[0]], axis=0))
    gram_out[0] = line
    gram_in[0] = line
    chips = n_gx * n_gy // 2
    columns = n_gy // 2
    for row in sorted(range(n_gx), key=lambda row: -min(row, n_gx - row)):
        first = row * columns
        each(max(first, 1), first + columns, lambda step: gram_copy(step).start())
    each(0, ITERS, sent)
    for i in range(8):
        cell_copy(i).wait_send()
    pair_copy().wait_send()
    bytes_of(gram_in.at[pl.ds(1, chips - 1)], gram_recv.at[0]).wait()
    line = merged(gram_in[...].reshape(chips, LANES))

    gram = [[None] * ITERS for a in range(ITERS)]
    for i, (a, b) in enumerate(pairs):
        gram[a][b] = line[:, i : i + 1]
    rho = mixed_coefficients(gram)
    mixed = rho[1] * y[1]
    for k in range(2, ITERS + 1):
        mixed = mixed + rho[k] * y[k]
    out_ref[...] = mixed

    bytes_of(gram_in.at[pl.ds(1, chips - 1)], gram_send.at[0]).wait()


def per_device(
    n_gx,
    n_gy,
    start_charges,
    solute_field,
    exposure,
    owner_offset,
    owner_row,
    live_slots,
    coupling,
    cell_index,
    evaluation,
    projection,
    far_kernel,
):
    hbm = pl.BlockSpec(memory_space=pl.ANY)
    piece = LANES // n_gy
    rows = piece + max(1, piece // Q)
    dma = pltpu.SemaphoreType.DMA

    def held(*shape, dtype=F32):
        return pltpu.VMEM(shape, dtype)

    return pl.pallas_call(
        functools.partial(kernel, n_gx, n_gy),
        out_shape=jax.ShapeDtypeStruct((SPH, H), F32),
        in_specs=[hbm] * 11,
        out_specs=pl.BlockSpec(memory_space=pltpu.VMEM),
        scratch_shapes=[
            held(SPH, H),
            held(SPH, H),
            held(NB, SPH, dtype=jnp.int32),
            held(NB, SPH, dtype=jnp.int32),
            held(ND, SPH, dtype=jnp.int32),
            held(NB, SPH),
            held(1, SPH, dtype=jnp.int32),
            held(ND * H, H),
            held(H, H),
            held(NC, NC),
            held(ITERS + 1, SPH, H),
            held(ITERS + 1, SPH, H),
            held(SPH, LANES),
            held(ND * SPH, SRC, dtype=BF16),
            held(ND * SPH, SRC, dtype=BF16),
            held(SRC, 2 * H, dtype=BF16),
            held(NC, SPH, dtype=BF16),
            held(NC, SPH, dtype=BF16),
            held(NC, NC, dtype=BF16),
            held(NC, NC, dtype=BF16),
            held(NC, SRC, dtype=BF16),
            held(NC, SRC, dtype=BF16),
            held(9, 1, LANES),
            held(ITERS, 8 * EDGE, H),
            held(ITERS, n_gy, rows, LANES),
            held(ITERS, n_gy, rows, LANES),
            held(ITERS, rows, LANES),
            held(ITERS, n_gx, rows, LANES),
            held(ITERS, n_gy, rows, LANES),
            held(Q, NC),
            held(1, NC),
            held(Q, NC),
            held(Q, NC),
            held(ITERS - 1, SPH, H),
            held(1, 1, LANES),
            held(1, 1, LANES),
            held(1, 1, LANES),
            held(n_gx * n_gy // 2, 1, LANES),
            dma((12,)),
            dma((ITERS, 8)),
            dma((ITERS, 8)),
            dma((8,)),
            dma((8,)),
            dma((ITERS,)),
            dma((ITERS,)),
            dma((ITERS,)),
            dma((ITERS,)),
            dma((ITERS,)),
            dma((ITERS,)),
            dma((2,)),
            dma((2,)),
        ],
        compiler_params=pltpu.CompilerParams(
            collective_id=0, has_side_effects=True, vmem_limit_bytes=48 * 1024 * 1024
        ),
        name="screening",
    )(
        *[
            pltpu.with_memory_space_constraint(a, pltpu.HBM)
            for a in (
        start_charges,
        solute_field,
        exposure,
        owner_offset.T,
        owner_row.T,
        live_slots.T,
        coupling.T,
        cell_index.reshape(1, SPH),
        evaluation,
        projection,
        far_kernel,
            )
        ]
    )


def solution(mesh):
    placed = (
        P(("gx", "gy"), None),
        P(("gx", "gy"), None),
        P(("gx", "gy"), None),
        P(("gx", "gy"), None),
        P(("gx", "gy"), None),
        P(("gx", "gy"), None),
        P(("gx", "gy"), None),
        P(("gx", "gy")),
        P(),
        P(),
        P(),
    )
    return jax.shard_map(
        functools.partial(per_device, mesh.shape["gx"], mesh.shape["gy"]),
        mesh=mesh,
        in_specs=placed,
        out_specs=P(("gx", "gy"), None),
        check_vma=False,
    )
```
